32 devices in a mesh: head: 2 (over y), seq: 16 (over z, x, core).
Axes of the slice: x: 2, y: 2, z: 4, core: 2. Of those that a mesh axis runs over, the one named last changes fastest.
Arguments:
- queries: bfloat16 [2, 8192, 2, 256], P(None, 'seq', 'head'), may hold values from -5 to 5
- key_rows: bfloat16 [2, 8192, 2, 256], P(None, 'seq', 'head'), may hold values from -5 to 5
- values: bfloat16 [2, 8192, 2, 256], P(None, 'seq', 'head'), may hold values from -6 to 6
- learn_rates: float32 [2, 2, 8192], P('head', None, 'seq'), may hold values from 0.02 to 0.6, as said below
- fast_gate: float32 [2, 256, 512], P('head'), may hold values from -0.375 to 0.375
- fast_down: float32 [2, 512, 256], P('head'), may hold values from -0.25 to 0.25
- fast_up: float32 [2, 256, 512], P('head'), may hold values from -0.375 to 0.375
- output_weight: bfloat16 [512, 512], P(None, ('head', 'seq')), may hold values from -0.25 to 0.25
Outputs:
- output: bfloat16 [2, 8192, 512], P(None, 'seq', 'head')
The draws below stay inside these ranges and needn't reach their ends.
Inputs may be any that keep to these rules, and one draw needn't show every extreme that they name: `learn_rates`: learning rates are positive.
All inputs are finite; a program needn't handle non-finite values.
Results may differ from the reference program's by a relative error of at most 0.0095.
Values may be sent and summed in bfloat16 or wider, within the bound.
A program may use at most 64 MiB of HBM per device.

```python
import math
import jax
import jax.numpy as jnp
from jax import lax

DH = 256
HID = 512
WINDOW = 256
SPANS = 2
SPAN_DEV = 512
HEADS = 2
D = 512
SPAN = 8192


def drawn_pair(key):
    base_key = jax.random.fold_in(key, 7001)
    subkeys = jax.random.split(base_key, 2)
    full_shape = (SPANS, SPAN, HEADS, DH)
    query_part = jnp.clip(jax.random.normal(subkeys[0], full_shape, jnp.float32), -4.0, 4.0)
    key_part = jnp.clip(jax.random.normal(subkeys[1], full_shape, jnp.float32), -4.0, 4.0)
    return (query_part, key_part)


def draw_queries(key, part):
    return drawn_pair(key)[0].astype(jnp.bfloat16)


def draw_key_rows(key, part):
    return drawn_pair(key)[1].astype(jnp.bfloat16)


def draw_learn_rates(key, part):
    base_key = jax.random.fold_in(key, 7013)
    full_shape = (HEADS, SPANS, SPAN)
    levels = jnp.exp(jax.random.uniform(base_key, full_shape, jnp.float32, math.log(0.02), math.log(0.2)))
    ramp_up = jnp.exp(math.log(3.0) * jnp.arange(SPAN, dtype=jnp.float32) / (SPAN - 1))
    return (levels * ramp_up).astype(jnp.float32)


def block_scale(own_key, shape, pieces, smallest, top_value):
    gain = 1.0
    for dim, parts in pieces:
        steps = jax.random.uniform(jax.random.fold_in(jax.random.fold_in(own_key, 6), dim), (parts,), jnp.float32, smallest / len(pieces), top_value / len(pieces))
        gain = gain * jnp.repeat(jnp.exp(steps), shape[dim] // parts).reshape((-1,) + (1,) * (len(shape) - 1 - dim))
    return gain


def gaussian(own_key, dims, deviation, most, cuts=(), kind=jnp.bfloat16):
    entries = jax.random.normal(own_key, dims, jnp.float32) * deviation
    if len(cuts) > 0:
        entries = block_scale(own_key, dims, cuts, -0.22, 0.18) * entries
    return jnp.clip(entries, min=-most, max=most).astype(kind)


def setup_inputs(seed: int = 0) -> dict:
    streams_of = jax.random.split(jax.random.key(seed), 9)
    queries = draw_queries(jax.random.fold_in(streams_of[8], 71), 0)
    key_rows = draw_key_rows(jax.random.fold_in(streams_of[8], 71), 0)
    values = gaussian(streams_of[2], (SPANS, SPAN, HEADS, DH), 1.0, 6.0, ((1, 16), (2, 2)))
    learn_rates = draw_learn_rates(jax.random.fold_in(streams_of[8], 71), 0)
    fast_gate = gaussian(streams_of[4], (HEADS, DH, HID), DH ** -0.5, 0.375, ((0, 2),), jnp.float32)
    fast_down = gaussian(streams_of[5], (HEADS, HID, DH), HID ** -0.5, 0.25, ((0, 2),), jnp.float32)
    fast_up = gaussian(streams_of[6], (HEADS, DH, HID), DH ** -0.5, 0.375, ((0, 2),), jnp.float32)
    output_weight = gaussian(streams_of[7], (D, D), D ** -0.5, 0.25, ((1, 32),))
    return {"queries": queries, "key_rows": key_rows, "values": values, "learn_rates": learn_rates, "fast_gate": fast_gate, "fast_down": fast_down, "fast_up": fast_up, "output_weight": output_weight}


MOMENTUM = 0.9

def silu_slope(pre_act):
    sigmoid_value = jax.nn.sigmoid(pre_act)
    return sigmoid_value * (1.0 + pre_act * (1.0 - sigmoid_value))

def span_gradient(key_span, value_span, rate_span, current):
    gate_low, down_low, up_low = current
    pre_gate = jnp.dot(key_span, gate_low, preferred_element_type=jnp.float32)
    pre_up = jnp.dot(key_span, up_low, preferred_element_type=jnp.float32)
    hidden = (jax.nn.silu(pre_gate) * pre_up).astype(jnp.bfloat16)
    target = (-(rate_span[:, None] * value_span.astype(jnp.float32))).astype(jnp.bfloat16)
    grad_down = jnp.dot(hidden.T, target, preferred_element_type=jnp.float32)
    back_grad = jnp.dot(target, down_low.T, preferred_element_type=jnp.float32)
    grad_pre_gate = (back_grad * pre_up * silu_slope(pre_gate)).astype(jnp.bfloat16)
    grad_pre_up = (back_grad * jax.nn.silu(pre_gate)).astype(jnp.bfloat16)
    grad_gate = jnp.dot(key_span.T, grad_pre_gate, preferred_element_type=jnp.float32)
    grad_up = jnp.dot(key_span.T, grad_pre_up, preferred_element_type=jnp.float32)
    return (grad_gate, grad_down, grad_up)

def apply_fast(query_span, current):
    gate_low, down_low, up_low = current
    pre_gate = jnp.dot(query_span, gate_low, preferred_element_type=jnp.float32)
    pre_up = jnp.dot(query_span, up_low, preferred_element_type=jnp.float32)
    hidden = (jax.nn.silu(pre_gate) * pre_up).astype(jnp.bfloat16)
    fast = jnp.dot(hidden, down_low, preferred_element_type=jnp.float32)
    return fast * lax.rsqrt(lax.optimization_barrier(jnp.mean(fast * fast, axis=-1, keepdims=True)) + 1e-05)

def fast_head(query_head, key_head, value_head, rate_head, gate_init, down_init, up_init):
    clip_bound = 0.6 * math.sqrt(HID)
    weights = (gate_init, down_init, up_init)
    current = tuple((matrix.astype(jnp.bfloat16) for matrix in weights))
    momentum = None
    results = []
    for span_index in range(SPANS):
        gradient = span_gradient(key_head[span_index], value_head[span_index], rate_head[span_index], current)
        squares = jnp.sum(gradient[0] * gradient[0]) + jnp.sum(gradient[1] * gradient[1]) + jnp.sum(gradient[2] * gradient[2])
        factor = jnp.minimum(1.0, clip_bound / jnp.sqrt(squares + 1e-06))
        if momentum is None:
            momentum = tuple((factor * member for member in gradient))
        else:
            momentum = tuple((MOMENTUM * earlier + factor * member for earlier, member in zip(momentum, gradient)))
        weights = tuple((matrix - change for matrix, change in zip(weights, momentum)))
        current = tuple((matrix.astype(jnp.bfloat16) for matrix in weights))
        results.append(apply_fast(query_head[span_index], current))
    return jnp.stack(results)

def window_head(query_flat, key_flat, value_flat):
    length = query_flat.shape[0]
    block_size = SPAN_DEV
    pad_keys = jnp.concatenate([jnp.zeros((WINDOW, DH), key_flat.dtype), key_flat], axis=0)
    pad_values = jnp.concatenate([jnp.zeros((WINDOW, DH), value_flat.dtype), value_flat], axis=0)
    row_ids = jnp.arange(block_size, dtype=jnp.int32)[:, None]
    col_ids = jnp.arange(block_size + WINDOW, dtype=jnp.int32)[None, :]
    in_band = (col_ids > row_ids) & (col_ids <= row_ids + WINDOW)
    score_scale = 1.0 / math.sqrt(DH)

    def one_block(block_index):
        offset = (block_index * block_size).astype(jnp.int32)
        query_rows = lax.dynamic_slice_in_dim(query_flat, offset, block_size, 0)
        key_block = lax.dynamic_slice_in_dim(pad_keys, offset, block_size + WINDOW, 0)
        value_block = lax.dynamic_slice_in_dim(pad_values, offset, block_size + WINDOW, 0)
        scores = jnp.dot(query_rows, key_block.T, preferred_element_type=jnp.float32) * score_scale
        allowed = in_band & (offset + col_ids >= WINDOW)
        scores = jnp.where(allowed, scores, -1e+30)
        row_max = lax.optimization_barrier(jnp.max(scores, axis=1, keepdims=True))
        exponent = jnp.exp(scores - row_max)
        probability = (exponent / lax.optimization_barrier(jnp.sum(exponent, axis=1, keepdims=True))).astype(jnp.bfloat16)
        return jnp.dot(probability, value_block, preferred_element_type=jnp.float32)
    blocks_out = lax.map(one_block, jnp.arange(length // block_size, dtype=jnp.int32))
    return blocks_out.reshape(length, DH)

def reference(queries, key_rows, values, learn_rates, fast_gate, fast_down, fast_up, output_weight):
    length = SPANS * SPAN
    mixed_heads = []
    for head_index in range(HEADS):
        query_head = queries[:, :, head_index]
        key_head = key_rows[:, :, head_index]
        value_head = values[:, :, head_index]
        fast_out = fast_head(query_head, key_head, value_head, learn_rates[head_index], fast_gate[head_index], fast_down[head_index], fast_up[head_index])
        window_out = window_head(query_head.reshape(length, DH), key_head.reshape(length, DH), value_head.reshape(length, DH))
        mixed_heads.append((fast_out.reshape(length, DH) + window_out).astype(jnp.bfloat16))
    joined = jnp.concatenate(mixed_heads, axis=1)
    result = jnp.dot(joined, output_weight, preferred_element_type=jnp.float32).astype(jnp.bfloat16)
    return result.reshape(SPANS, SPAN, D)
```

```python
import functools
import math

import jax
import jax.numpy as jnp
from jax import lax
from jax.experimental import pallas as pl
from jax.experimental.pallas import tpu as pltpu
from jax.sharding import PartitionSpec as P

WINDOW = 256
MOMENTUM = 0.9
LANES = 128
MESH = pl.DeviceIdType.MESH
F32 = jnp.float32
BF16 = jnp.bfloat16


def radices_of(count):
    found = []
    while count > 1:
        if count % 2:
            found.append(count)
        elif len(found) < 2 or count % 4:
            found.append(2)
        else:
            found.append(4)
        count //= found[-1]
    return found


def dot(left, right):
    return jnp.dot(left, right, preferred_element_type=F32)


def dot_t(left, right):
    return lax.dot_general(left, right, (((1,), (1,)), ((), ())), preferred_element_type=F32)


def sigmoid(value):
    return 0.5 * jnp.tanh(0.5 * value) + 0.5


def kernel(
    n_seq, n_head, gather_weight,
    q_ref, k_ref, v_ref, rate_ref, gate_ref, down_ref, up_ref, ow_ref,
    out_ref,
    wts, mom, gate_b, up_b, down_tb, keys_t, target, target_t, hid_s, da_s, db_s,
    acc, send_b, recv_b, full_b, edge_k, edge_v, ow_all, ow_t, mix, win,
    ar_send, ar_recv, ag_send, ag_recv, halo_send, halo_recv, ow_send, ow_recv, mix_send, mix_recv,
):
    spans, rows, dh = q_ref.shape
    hid = gate_ref.shape[1]
    cols = hid // LANES
    blocks = 3 * cols
    total = blocks * dh
    radices = radices_of(n_seq)
    levels = len(radices)
    me = lax.axis_index("seq")
    head = lax.axis_index("head")

    strides, digits = [], []
    stride = 1
    for radix in radices:
        strides.append(stride)
        digits.append(lax.rem(me // stride, radix))
        stride *= radix

    def peer(level, step):
        radix = radices[level]
        other = lax.rem(digits[level] + step, radix)
        return me + (other - digits[level]) * strides[level], other

    following = lax.rem(me + 1, n_seq)
    before = lax.rem(me + n_seq - 1, n_seq)

    barrier = pltpu.get_barrier_semaphore()
    greeted = 0
    for level in range(levels):
        for step in range(1, radices[level]):
            pl.semaphore_signal(barrier, inc=1, device_id={"seq": peer(level, step)[0]}, device_id_type=MESH)
            greeted += 1
    for other in (following, before):
        pl.semaphore_signal(barrier, inc=1, device_id={"seq": other}, device_id_type=MESH)
        greeted += 1
    for step in range(1, n_head):
        pl.semaphore_signal(
            barrier, inc=1, device_id={"head": lax.rem(head + step, n_head)}, device_id_type=MESH
        )
        greeted += 1

    def prepare(c):
        rate_row = jnp.broadcast_to(rate_ref[c : c + 1, :], (LANES, rows))
        rate = rate_row.T
        rate = jnp.concatenate([rate] * (dh // LANES), axis=1)
        aim = (-(rate * v_ref[c].astype(F32))).astype(BF16)
        target[...] = aim
        target_t[...] = aim.T
        keys_t[...] = k_ref[c].T

    def set_current(index, m, cb):
        dest = (gate_b, down_tb, up_b)[m]
        dest[:, cb * LANES : (cb + 1) * LANES] = wts[index].astype(BF16)

    down_t = down_ref[...].T
    for m in range(3):
        for cb in range(cols):
            lanes = slice(cb * LANES, (cb + 1) * LANES)
            block = down_t[:, lanes] if m == 1 else (gate_ref, None, up_ref)[m][:, lanes]
            wts[m * cols + cb] = block
            set_current(m * cols + cb, m, cb)

    def gradient(c):
        piece = min(256, rows)
        for start in range(0, rows, piece):
            part = slice(start, start + piece)
            k_part = k_ref[c, part]
            pre_gate = dot(k_part, gate_b[...])
            pre_up = dot(k_part, up_b[...])
            back = dot(target[part, :], down_tb[...])
            sig = sigmoid(pre_gate)
            silu = pre_gate * sig
            hid_s[part, :] = (silu * pre_up).astype(BF16)
            da_s[part, :] = (back * pre_up * (sig * (1.0 + pre_gate * (1.0 - sig)))).astype(BF16)
            db_s[part, :] = (back * silu).astype(BF16)
        for m, (left, right) in enumerate(((keys_t, da_s), (target_t, hid_s), (keys_t, db_s))):
            grad = dot(left[...], right[...])
            for cb in range(cols):
                base = (m * cols + cb) * dh
                block = grad[:, cb * LANES : (cb + 1) * LANES]
                acc[base : base + dh, :] = block
                send_b[c, base : base + dh, :] = block.astype(BF16)

    def span_of(start, size):
        return pl.ds(pl.multiple_of(start, 16), size)

    def fill(work):
        if work:
            work.pop(0)()

    def gather_copies(buf, unit, level, sends, recvs):
        size = unit * math.prod(radices[level + 1 :])
        start = 0
        for l in range(level + 1):
            start = start + digits[l] * (unit * math.prod(radices[l + 1 :]))
        made = []
        for step in range(1, radices[level]):
            slot = sum(radices[:level]) + step
            block = buf.at[span_of(start, size)]
            made.append(
                pltpu.make_async_remote_copy(
                    src_ref=block, dst_ref=block, send_sem=sends.at[slot], recv_sem=recvs.at[slot],
                    device_id={"seq": peer(level, step)[0]}, device_id_type=MESH,
                )
            )
        return made

    def all_reduce(c, work):
        pending = []
        size = total
        base = 0
        slot_base = 0
        for level in range(levels):
            size //= radices[level]
            copies = []
            for step in range(1, radices[level]):
                target_dev, other = peer(level, step)
                slot = sum(radices[:level]) + step
                copy = pltpu.make_async_remote_copy(
                    src_ref=send_b.at[c, span_of(base + other * size, size)],
                    dst_ref=recv_b.at[c, pl.ds(slot_base + (step - 1) * size, size)],
                    send_sem=ar_send.at[c, slot], recv_sem=ar_recv.at[c, slot],
                    device_id={"seq": target_dev}, device_id_type=MESH,
                )
                copy.start()
                copies.append(copy)
            fill(work)
            base = base + digits[level] * size
            for copy in copies:
                copy.wait_recv()
            pending += copies
            mine = acc[span_of(base, size), :]
            for step in range(1, radices[level]):
                mine += recv_b[c, slot_base + (step - 1) * size : slot_base + step * size, :].astype(F32)
            slot_base += (radices[level] - 1) * size
            if level < levels - 1:
                acc[span_of(base, size), :] = mine
                send_b[c, span_of(base, size), :] = mine.astype(BF16)
            else:
                full_b[c, span_of(base, size), :] = mine.astype(BF16)
        for level in reversed(range(levels)):
            copies = gather_copies(full_b.at[c], total // n_seq, level, ag_send.at[c], ag_recv.at[c])
            for copy in copies:
                copy.start()
            fill(work)
            for copy in copies:
                copy.wait_recv()
            pending += copies
        while work:
            fill(work)
        for copy in pending:
            copy.wait_send()

    def update(c):
        squares = jnp.zeros((8, LANES), F32)
        for index in range(blocks):
            block = full_b[c, index * dh : (index + 1) * dh, :].astype(F32)
            squares += jnp.sum((block * block).reshape(dh // 8, 8, LANES), axis=0)
        whole = jnp.sum(jnp.sum(squares, axis=1, keepdims=True), axis=0, keepdims=True)
        factor = jnp.minimum(1.0, 0.6 * math.sqrt(hid) / jnp.sqrt(whole + 1e-6))
        for m in range(3):
            for cb in range(cols):
                index = m * cols + cb
                change = factor * full_b[c, index * dh : (index + 1) * dh, :].astype(F32)
                if c > 0:
                    change = MOMENTUM * mom[index] + change
                if c < spans - 1:
                    mom[index] = change
                wts[index] = wts[index] - change
                set_current(index, m, cb)

    row_ids = lax.broadcasted_iota(jnp.int32, (WINDOW, WINDOW), 0)
    col_ids = lax.broadcasted_iota(jnp.int32, (WINDOW, WINDOW), 1)
    scale = 1.0 / math.sqrt(dh)

    def attend(c, j):
        start = j * WINDOW
        here = slice(start, start + WINDOW)
        left_ok = col_ids > row_ids
        if j == 0:
            first = me == 0
            span = jnp.where(first, (c + spans - 1) % spans, c)
            left_k, left_v = edge_k[span], edge_v[span]
            if c == 0:
                left_ok = left_ok & jnp.logical_not(first)
        else:
            earlier = slice(start - WINDOW, start)
            left_k, left_v = k_ref[c, earlier], v_ref[c, earlier]
        query = q_ref[c, here]
        left = jnp.where(left_ok, dot_t(query, left_k) * scale, -1e30)
        right = jnp.where(col_ids <= row_ids, dot_t(query, k_ref[c, here]) * scale, -1e30)
        top = jnp.maximum(jnp.max(left, axis=1, keepdims=True), jnp.max(right, axis=1, keepdims=True))
        left = jnp.exp(left - top)
        right = jnp.exp(right - top)
        share = 1.0 / (jnp.sum(left, axis=1, keepdims=True) + jnp.sum(right, axis=1, keepdims=True))
        win[c, here] = dot((left * share).astype(BF16), left_v) + dot(
            (right * share).astype(BF16), v_ref[c, here]
        )

    half = WINDOW

    def mix_copies(c, j):
        made = []
        for step in range(1, n_head):
            block = mix.at[head, c, pl.ds(j * half, half)]
            made.append(
                pltpu.make_async_remote_copy(
                    src_ref=block, dst_ref=block,
                    send_sem=mix_send.at[c, j, step], recv_sem=mix_recv.at[c, j, step],
                    device_id={"head": lax.rem(head + step, n_head)}, device_id_type=MESH,
                )
            )
        return made

    def apply(c, j):
        part = slice(j * half, (j + 1) * half)
        query = q_ref[c, part]
        pre_gate = dot(query, gate_b[...])
        hidden = (pre_gate * sigmoid(pre_gate) * dot(query, up_b[...])).astype(BF16)
        fast = dot_t(hidden, down_tb[...])
        norm = fast * lax.rsqrt(jnp.mean(fast * fast, axis=-1, keepdims=True) + 1e-5)
        mix[head, c, part] = (norm + win[c, part]).astype(BF16)
        for copy in mix_copies(c, j):
            copy.start()

    def project(c, j):
        part = slice(j * half, (j + 1) * half)
        for copy in mix_copies(c, j):
            copy.wait()
        result = None
        for h in range(n_head):
            term = dot_t(mix[h, c, part], ow_t[:, h * dh : (h + 1) * dh])
            result = term if result is None else result + term
        out_ref[c, part] = result.astype(BF16)

    halo = []
    for index, (source, dest) in enumerate(((k_ref, edge_k), (v_ref, edge_v))):
        for c in range(spans):
            halo.append(
                pltpu.make_async_remote_copy(
                    src_ref=source.at[c, pl.ds(rows - WINDOW, WINDOW)], dst_ref=dest.at[c],
                    send_sem=halo_send.at[index, c], recv_sem=halo_recv.at[index, c],
                    device_id={"seq": following}, device_id_type=MESH,
                )
            )

    def halo_wait():
        for copy in halo:
            copy.wait()

    shard = ow_ref.shape[0]
    if gather_weight:
        mine = 0
        for l in range(levels):
            mine = mine + digits[l] * (shard * math.prod(radices[l + 1 :]))
        ow_all[span_of(mine, shard), :] = ow_ref[...]

    def weight_start(level):
        if gather_weight:
            for copy in gather_copies(ow_all, shard, level, ow_send, ow_recv):
                copy.start()

    def weight_wait(level):
        if gather_weight:
            for copy in gather_copies(ow_all, shard, level, ow_send, ow_recv):
                copy.wait()

    def weight_end():
        if not gather_weight:
            ow_t[...] = ow_ref[...]
            return
        weight_wait(0)
        for s in range(n_seq):
            place, rest = 0, s
            for radix in radices:
                place = place * radix + rest % radix
                rest //= radix
            ow_t[s * shard : (s + 1) * shard, :] = ow_all[place * shard : (place + 1) * shard, :]

    tiles = rows // WINDOW
    prepare(0)
    pl.semaphore_wait(barrier, greeted)
    for copy in halo:
        copy.start()
    gradient(0)
    for c in range(spans):
        work = []
        if c + 1 < spans:
            work.append(functools.partial(prepare, c + 1))
        if c == 0:
            work += [functools.partial(attend, s, j) for s in range(spans) for j in range(1, tiles)]

            def edges():
                halo_wait()
                attend(0, 0)

            work.append(edges)
            work += [functools.partial(attend, s, 0) for s in range(1, spans)]
        if c == spans - 1:
            for level in reversed(range(levels)):
                def step(level=level):
                    if level < levels - 1:
                        weight_wait(level + 1)
                    weight_start(level)
                    for j in range(tiles):
                        if j % levels == levels - 1 - level and c > 0:
                            apply(c - 1, j)
                work.append(step)

            def last():
                weight_end()
                if c > 0:
                    for j in range(tiles):
                        project(c - 1, j)

            work.append(last)
        elif c > 0:
            for j in range(tiles):
                work.append(functools.partial(apply, c - 1, j))
            for j in range(tiles):
                work.append(functools.partial(project, c - 1, j))
        all_reduce(c, work)
        update(c)
        if c + 1 < spans:
            gradient(c + 1)
    for j in range(tiles):
        apply(spans - 1, j)
    for j in range(tiles):
        project(spans - 1, j)


def body(n_seq, n_head, queries, key_rows, values, learn_rates, fast_gate, fast_down, fast_up, output_weight):
    spans, rows, _, dh = queries.shape
    hid = fast_gate.shape[2]
    features, shard = output_weight.shape
    gather_weight = shard % 16 == 0
    if gather_weight:
        weight = output_weight.T
    else:
        weight = lax.all_gather(output_weight, "seq", axis=1, tiled=True).T
    out_cols = shard * n_seq
    cols = hid // LANES
    total = 3 * cols * dh
    radices = radices_of(n_seq)
    landing, size = 0, total
    for radix in radices:
        size //= radix
        landing += (radix - 1) * size
    slots = sum(radices) + 1
    tiles = rows // WINDOW
    dma = pltpu.SemaphoreType.DMA
    vmem = pltpu.VMEM
    return pl.pallas_call(
        functools.partial(kernel, n_seq, n_head, gather_weight),
        out_shape=jax.ShapeDtypeStruct((spans, rows, out_cols), BF16),
        in_specs=[pl.BlockSpec(memory_space=pltpu.VMEM)] * 8,
        out_specs=pl.BlockSpec(memory_space=pltpu.VMEM),
        scratch_shapes=[
            vmem((3 * cols, dh, LANES), F32),
            vmem((3 * cols, dh, LANES), F32),
            vmem((dh, hid), BF16),
            vmem((dh, hid), BF16),
            vmem((dh, hid), BF16),
            vmem((dh, rows), BF16),
            vmem((rows, dh), BF16),
            vmem((dh, rows), BF16),
            vmem((rows, hid), BF16),
            vmem((rows, hid), BF16),
            vmem((rows, hid), BF16),
            vmem((total, LANES), F32),
            vmem((spans, total, LANES), BF16),
            vmem((spans, landing, LANES), BF16),
            vmem((spans, total, LANES), BF16),
            vmem((spans, WINDOW, dh), BF16),
            vmem((spans, WINDOW, dh), BF16),
            vmem((out_cols, features), BF16),
            vmem((out_cols, features), BF16),
            vmem((n_head, spans, rows, dh), BF16),
            vmem((spans, rows, dh), F32),
            dma((spans, slots)),
            dma((spans, slots)),
            dma((spans, slots)),
            dma((spans, slots)),
            dma((2, spans)),
            dma((2, spans)),
            dma((slots,)),
            dma((slots,)),
            dma((spans, tiles, n_head)),
            dma((spans, tiles, n_head)),
        ],
        compiler_params=pltpu.CompilerParams(
            collective_id=0, has_side_effects=True, vmem_limit_bytes=48 * 1024 * 1024
        ),
    )(
        queries[:, :, 0, :], key_rows[:, :, 0, :], values[:, :, 0, :], learn_rates[0],
        fast_gate[0], fast_down[0], fast_up[0], weight,
    )


def solution(mesh):
    placed = (
        P(None, "seq", "head", None),
        P(None, "seq", "head", None),
        P(None, "seq", "head", None),
        P("head", None, "seq"),
        P("head", None, None),
        P("head", None, None),
        P("head", None, None),
        P(None, ("head", "seq")),
    )
    return jax.shard_map(
        functools.partial(body, mesh.shape["seq"], mesh.shape["head"]),
        mesh=mesh, in_specs=placed, out_specs=P(None, "seq", "head"), check_vma=False,
    )
```

```python
import functools
import math

import jax
import jax.numpy as jnp
from jax import lax
from jax.experimental import pallas as pl
from jax.experimental.pallas import tpu as pltpu
from jax.sharding import PartitionSpec as P

WINDOW = 256
MOMENTUM = 0.9
LANES = 128
MESH = pl.DeviceIdType.MESH
F32 = jnp.float32
BF16 = jnp.bfloat16


def radices_of(count):
    found = []
    while count > 1:
        if count % 2:
            found.append(count)
        elif len(found) < 2 or count % 4:
            found.append(2)
        else:
            found.append(4)
        count //= found[-1]
    return found


def dot(left, right):
    return jnp.dot(left, right, preferred_element_type=F32)


def dot_t(left, right):
    return lax.dot_general(left, right, (((1,), (1,)), ((), ())), preferred_element_type=F32)


def sigmoid(value):
    return 0.5 * jnp.tanh(0.5 * value) + 0.5


def kernel(
    n_seq, n_head, gather_weight,
    q_hbm, k_hbm, v_hbm, rate_hbm, gate_hbm, down_hbm, up_hbm, ow_hbm,
    out_ref,
    q_ref, k_ref, v_ref, rate_ref, gate_w, down_ref, up_w, ow_ref, down_w,
    mom, gate_b, up_b, down_tb, keys_t, target, target_t, hid_s, da_s, db_s,
    acc, send_b, recv_b, full_b, edge_k, edge_v, ow_all, ow_t, mix, win,
    load_sem, ar_send, ar_recv, ag_send, ag_recv, halo_send, halo_recv, ow_send, ow_recv, mix_send, mix_recv,
):
    spans, rows, dh = q_ref.shape
    hid = gate_w.shape[1]
    cols = hid // LANES
    part_rows = cols * dh
    wts = (gate_w, down_w, up_w)
    current = (gate_b, down_tb, up_b)
    radices = radices_of(n_seq)
    levels = len(radices)
    me = lax.axis_index("seq")
    head = lax.axis_index("head")

    loads = {}

    def load(name, source, dest):
        loads[name] = pltpu.make_async_copy(source, dest, load_sem.at[len(loads)])
        loads[name].start()

    load("gate", gate_hbm, gate_w)
    load(("k", 0), k_hbm.at[0], k_ref.at[0])
    load("up", up_hbm, up_w)
    load("rate", rate_hbm, rate_ref)
    load(("v", 0), v_hbm.at[0], v_ref.at[0])
    load("down", down_hbm, down_ref)
    load("ow", ow_hbm, ow_ref)
    for c in range(1, spans):
        load(("k", c), k_hbm.at[c], k_ref.at[c])
        load(("v", c), v_hbm.at[c], v_ref.at[c])
    load("q", q_hbm, q_ref)

    strides, digits = [], []
    stride = 1
    for radix in radices:
        strides.append(stride)
        digits.append(lax.rem(me // stride, radix))
        stride *= radix

    def peer(level, step):
        radix = radices[level]
        other = lax.rem(digits[level] + step, radix)
        return me + (other - digits[level]) * strides[level], other

    following = lax.rem(me + 1, n_seq)
    before = lax.rem(me + n_seq - 1, n_seq)

    barrier = pltpu.get_barrier_semaphore()
    greeted = 0
    for level in range(levels):
        for step in range(1, radices[level]):
            pl.semaphore_signal(barrier, inc=1, device_id={"seq": peer(level, step)[0]}, device_id_type=MESH)
            greeted += 1
    for other in (following, before):
        pl.semaphore_signal(barrier, inc=1, device_id={"seq": other}, device_id_type=MESH)
        greeted += 1
    for step in range(1, n_head):
        pl.semaphore_signal(
            barrier, inc=1, device_id={"head": lax.rem(head + step, n_head)}, device_id_type=MESH
        )
        greeted += 1

    def prepare(c):
        rate_row = jnp.broadcast_to(rate_ref[c : c + 1, :], (LANES, rows))
        rate = rate_row.T
        rate = jnp.concatenate([rate] * (dh // LANES), axis=1)
        aim = (-(rate * v_ref[c].astype(F32))).astype(BF16)
        target[...] = aim
        target_t[...] = aim.T
        keys_t[...] = k_ref[c].T

    def gradient(c):
        piece = min(256, rows)
        for start in range(0, rows, piece):
            part = slice(start, start + piece)
            k_part = k_ref[c, part]
            pre_gate = dot(k_part, gate_b[...])
            pre_up = dot(k_part, up_b[...])
            back = dot(target[part, :], down_tb[...])
            sig = sigmoid(pre_gate)
            silu = pre_gate * sig
            hid_s[part, :] = (silu * pre_up).astype(BF16)
            da_s[part, :] = (back * pre_up * (sig * (1.0 + pre_gate * (1.0 - sig)))).astype(BF16)
            db_s[part, :] = (back * silu).astype(BF16)
        for p, (left, right) in enumerate(((target_t, hid_s), (keys_t, da_s), (keys_t, db_s))):
            grad = dot(left[...], right[...])
            for cb in range(cols):
                base = p * part_rows + cb * dh
                block = grad[:, cb * LANES : (cb + 1) * LANES]
                acc[base : base + dh, :] = block
                send_b[c, base : base + dh, :] = block.astype(BF16)
            start_stage(c, p, 0)

    def span_of(start, size):
        return pl.ds(pl.multiple_of(start, 16), size)

    def fill(work):
        if work:
            work.pop(0)()

    def owned(unit, level):
        start = 0
        for l in range(level + 1):
            start = start + digits[l] * (unit * math.prod(radices[l + 1 :]))
        return start

    def gather_copies(buf, offset, unit, level, sends, recvs):
        size = unit * math.prod(radices[level + 1 :])
        made = []
        for step in range(1, radices[level]):
            slot = sum(radices[:level]) + step
            block = buf.at[span_of(offset + owned(unit, level), size)]
            made.append(
                pltpu.make_async_remote_copy(
                    src_ref=block, dst_ref=block, send_sem=sends.at[slot], recv_sem=recvs.at[slot],
                    device_id={"seq": peer(level, step)[0]}, device_id_type=MESH,
                )
            )
        return made

    unit = part_rows // n_seq

    def scatter_copies(c, p, level):
        size = unit * math.prod(radices[level + 1 :])
        base = p * part_rows + (owned(unit, level - 1) if level else 0)
        made = []
        for step in range(1, radices[level]):
            target_dev, other = peer(level, step)
            slot = sum(radices[:level]) + step
            made.append(
                pltpu.make_async_remote_copy(
                    src_ref=send_b.at[c, span_of(base + other * size, size)],
                    dst_ref=recv_b.at[c, pl.ds(landing_at(p, level) + (step - 1) * size, size)],
                    send_sem=ar_send.at[c, p, slot], recv_sem=ar_recv.at[c, p, slot],
                    device_id={"seq": target_dev}, device_id_type=MESH,
                )
            )
        return made

    def landing_at(p, level):
        sizes = [unit * math.prod(radices[l + 1 :]) * (radices[l] - 1) for l in range(levels)]
        return p * sum(sizes) + sum(sizes[:level])

    stages = 2 * levels

    def stage_copies(c, p, stage):
        if stage < levels:
            return scatter_copies(c, p, stage)
        return gather_copies(
            full_b.at[c], p * part_rows, unit, stages - 1 - stage, ag_send.at[c, p], ag_recv.at[c, p]
        )

    def start_stage(c, p, stage):
        for copy in stage_copies(c, p, stage):
            copy.start()

    def finish_stage(c, p, stage):
        for copy in stage_copies(c, p, stage):
            copy.wait_recv()
        if stage < levels:
            size = unit * math.prod(radices[stage + 1 :])
            place = span_of(p * part_rows + owned(unit, stage), size)
            mine = acc[place, :]
            landed = landing_at(p, stage)
            for step in range(radices[stage] - 1):
                mine += recv_b[c, landed + step * size : landed + (step + 1) * size, :].astype(F32)
            if stage < levels - 1:
                acc[place, :] = mine
                send_b[c, place, :] = mine.astype(BF16)
            else:
                full_b[c, place, :] = mine.astype(BF16)
        if stage + 1 < stages:
            start_stage(c, p, stage + 1)

    def all_reduce(c, work):
        squares = jnp.zeros((8, LANES), F32)
        for p in range(3):
            finish_stage(c, p, 0)
        for key in range(1, stages + 2):
            fill(work)
            for p in reversed(range(3)):
                stage = key - p
                if 1 <= stage < stages:
                    finish_stage(c, p, stage)
                    if stage == stages - 1:
                        for cb in range(cols):
                            base = p * part_rows + cb * dh
                            block = full_b[c, base : base + dh, :].astype(F32)
                            squares += jnp.sum((block * block).reshape(dh // 8, 8, LANES), axis=0)
        while work:
            fill(work)
        for p in range(3):
            for stage in range(stages):
                for copy in stage_copies(c, p, stage):
                    copy.wait_send()
        return squares

    def update(c, squares):
        whole = jnp.sum(jnp.sum(squares, axis=1, keepdims=True), axis=0, keepdims=True)
        factor = jnp.minimum(1.0, 0.6 * math.sqrt(hid) / jnp.sqrt(whole + 1e-6))
        for p, m in ((1, 0), (2, 2), (0, 1)):
            for cb in range(cols):
                base = p * part_rows + cb * dh
                lanes = slice(cb * LANES, (cb + 1) * LANES)
                change = factor * full_b[c, base : base + dh, :].astype(F32)
                if c > 0:
                    change = MOMENTUM * mom[m, :, lanes] + change
                fresh = wts[m][:, lanes] - change
                if c < spans - 1:
                    mom[m, :, lanes] = change
                    wts[m][:, lanes] = fresh
                current[m][:, lanes] = fresh.astype(BF16)

    row_ids = lax.broadcasted_iota(jnp.int32, (WINDOW, WINDOW), 0)
    col_ids = lax.broadcasted_iota(jnp.int32, (WINDOW, WINDOW), 1)
    scale = 1.0 / math.sqrt(dh)

    def attend(c, j):
        start = j * WINDOW
        here = slice(start, start + WINDOW)
        left_ok = col_ids > row_ids
        if j == 0:
            first = me == 0
            span = jnp.where(first, (c + spans - 1) % spans, c)
            left_k, left_v = edge_k[span], edge_v[span]
            if c == 0:
                left_ok = left_ok & jnp.logical_not(first)
        else:
            earlier = slice(start - WINDOW, start)
            left_k, left_v = k_ref[c, earlier], v_ref[c, earlier]
        query = q_ref[c, here]
        left = jnp.where(left_ok, dot_t(query, left_k) * scale, -1e30)
        right = jnp.where(col_ids <= row_ids, dot_t(query, k_ref[c, here]) * scale, -1e30)
        top = jnp.maximum(jnp.max(left, axis=1, keepdims=True), jnp.max(right, axis=1, keepdims=True))
        left = jnp.exp(left - top)
        right = jnp.exp(right - top)
        share = 1.0 / (jnp.sum(left, axis=1, keepdims=True) + jnp.sum(right, axis=1, keepdims=True))
        win[c, here] = dot((left * share).astype(BF16), left_v) + dot(
            (right * share).astype(BF16), v_ref[c, here]
        )

    half = WINDOW

    def mix_copies(c, j):
        made = []
        for step in range(1, n_head):
            block = mix.at[head, c, pl.ds(j * half, half)]
            made.append(
                pltpu.make_async_remote_copy(
                    src_ref=block, dst_ref=block,
                    send_sem=mix_send.at[c, j, step], recv_sem=mix_recv.at[c, j, step],
                    device_id={"head": lax.rem(head + step, n_head)}, device_id_type=MESH,
                )
            )
        return made

    def apply(c, j):
        part = slice(j * half, (j + 1) * half)
        query = q_ref[c, part]
        pre_gate = dot(query, gate_b[...])
        hidden = (pre_gate * sigmoid(pre_gate) * dot(query, up_b[...])).astype(BF16)
        fast = dot_t(hidden, down_tb[...])
        norm = fast * lax.rsqrt(jnp.mean(fast * fast, axis=-1, keepdims=True) + 1e-5)
        mix[head, c, part] = (norm + win[c, part]).astype(BF16)
        for copy in mix_copies(c, j):
            copy.start()

    def project(c, j):
        part = slice(j * half, (j + 1) * half)
        for copy in mix_copies(c, j):
            copy.wait()
        result = None
        for h in range(n_head):
            term = dot_t(mix[h, c, part], ow_t[:, h * dh : (h + 1) * dh])
            result = term if result is None else result + term
        out_ref[c, part] = result.astype(BF16)

    halo = []
    for index, (source, dest) in enumerate(((k_hbm, edge_k), (v_hbm, edge_v))):
        for c in range(spans):
            halo.append(
                pltpu.make_async_remote_copy(
                    src_ref=source.at[c, pl.ds(rows - WINDOW, WINDOW)], dst_ref=dest.at[c],
                    send_sem=halo_send.at[index, c], recv_sem=halo_recv.at[index, c],
                    device_id={"seq": following}, device_id_type=MESH,
                )
            )

    shard = ow_ref.shape[0]

    def weight_copies(level):
        return gather_copies(ow_all, 0, shard, level, ow_send, ow_recv)

    def weight_next(level):
        if level < levels - 1:
            for copy in weight_copies(level + 1):
                copy.wait()
        for copy in weight_copies(level):
            copy.start()

    def weight_end():
        for copy in weight_copies(0):
            copy.wait()
        for s in range(n_seq):
            place, rest = 0, s
            for radix in radices:
                place = place * radix + rest % radix
                rest //= radix
            ow_t[s * shard : (s + 1) * shard, :] = ow_all[place * shard : (place + 1) * shard, :]

    tiles = rows // WINDOW
    pl.semaphore_wait(barrier, greeted)
    for copy in halo:
        copy.start()
    loads["gate"].wait()
    gate_b[...] = gate_w[...].astype(BF16)
    loads["up"].wait()
    up_b[...] = up_w[...].astype(BF16)
    loads["down"].wait()
    down_w[...] = down_ref[...].T
    down_tb[...] = down_w[...].astype(BF16)
    loads["rate"].wait()
    loads[("k", 0)].wait()
    loads[("v", 0)].wait()
    prepare(0)
    loads["ow"].wait()
    if gather_weight:
        ow_all[span_of(owned(shard, levels - 1), shard), :] = ow_ref[...]
        weight_next(levels - 1)
    else:
        ow_t[...] = ow_ref[...]
    gradient(0)
    loads["q"].wait()
    for c in range(1, spans):
        loads[("k", c)].wait()
        loads[("v", c)].wait()
    for c in range(spans):
        work = []
        if c + 1 < spans:
            work.append(functools.partial(prepare, c + 1))
        if c == 0:
            work += [functools.partial(attend, s, j) for s in range(spans) for j in range(1, tiles)]

            def edges():
                for copy in halo:
                    copy.wait()
                attend(0, 0)

            work.append(edges)
            work += [functools.partial(attend, s, 0) for s in range(1, spans)]
        if c > 0:
            work += [functools.partial(apply, c - 1, j) for j in range(tiles)]
        if c == spans - 1:
            if gather_weight:
                first = levels - 2 if c > 0 else levels - 1
                work += [functools.partial(weight_next, level) for level in reversed(range(first))]
                work.append(weight_end)
            work += [functools.partial(project, s, j) for s in range(c) for j in range(tiles)]
        update(c, all_reduce(c, work))
        if c + 1 < spans:
            if c + 1 == spans - 1 and gather_weight and levels > 1:
                weight_next(levels - 2)
            gradient(c + 1)
    for j in range(tiles):
        apply(spans - 1, j)
    for j in range(tiles):
        project(spans - 1, j)


def body(n_seq, n_head, queries, key_rows, values, learn_rates, fast_gate, fast_down, fast_up, output_weight):
    spans, rows, _, dh = queries.shape
    hid = fast_gate.shape[2]
    features, shard = output_weight.shape
    gather_weight = shard % 16 == 0
    if gather_weight:
        weight = output_weight.T
    else:
        weight = lax.all_gather(output_weight, "seq", axis=1, tiled=True).T
    out_cols = shard * n_seq
    cols = hid // LANES
    total = 3 * cols * dh
    radices = radices_of(n_seq)
    landing, size = 0, total
    for radix in radices:
        size //= radix
        landing += (radix - 1) * size
    slots = sum(radices) + 1
    tiles = rows // WINDOW
    dma = pltpu.SemaphoreType.DMA
    vmem = pltpu.VMEM
    return pl.pallas_call(
        functools.partial(kernel, n_seq, n_head, gather_weight),
        out_shape=jax.ShapeDtypeStruct((spans, rows, out_cols), BF16),
        in_specs=[pl.BlockSpec(memory_space=pltpu.HBM)] * 8,
        out_specs=pl.BlockSpec(memory_space=pltpu.VMEM),
        scratch_shapes=[
            vmem((spans, rows, dh), BF16),
            vmem((spans, rows, dh), BF16),
            vmem((spans, rows, dh), BF16),
            vmem((spans, rows), F32),
            vmem((dh, hid), F32),
            vmem((hid, dh), F32),
            vmem((dh, hid), F32),
            vmem(weight.shape, BF16),
            vmem((dh, hid), F32),
            vmem((3, dh, hid), F32),
            vmem((dh, hid), BF16),
            vmem((dh, hid), BF16),
            vmem((dh, hid), BF16),
            vmem((dh, rows), BF16),
            vmem((rows, dh), BF16),
            vmem((dh, rows), BF16),
            vmem((rows, hid), BF16),
            vmem((rows, hid), BF16),
            vmem((rows, hid), BF16),
            vmem((total, LANES), F32),
            vmem((spans, total, LANES), BF16),
            vmem((spans, landing, LANES), BF16),
            vmem((spans, total, LANES), BF16),
            vmem((spans, WINDOW, dh), BF16),
            vmem((spans, WINDOW, dh), BF16),
            vmem((out_cols, features), BF16),
            vmem((out_cols, features), BF16),
            vmem((n_head, spans, rows, dh), BF16),
            vmem((spans, rows, dh), F32),
            dma((6 + 2 * spans,)),
            dma((spans, 3, slots)),
            dma((spans, 3, slots)),
            dma((spans, 3, slots)),
            dma((spans, 3, slots)),
            dma((2, spans)),
            dma((2, spans)),
            dma((slots,)),
            dma((slots,)),
            dma((spans, tiles, n_head)),
            dma((spans, tiles, n_head)),
        ],
        compiler_params=pltpu.CompilerParams(
            collective_id=0, has_side_effects=True, vmem_limit_bytes=60 * 1024 * 1024
        ),
    )(
        queries[:, :, 0, :], key_rows[:, :, 0, :], values[:, :, 0, :], learn_rates[0],
        fast_gate[0], fast_down[0], fast_up[0], weight,
    )


def solution(mesh):
    placed = (
        P(None, "seq", "head", None),
        P(None, "seq", "head", None),
        P(None, "seq", "head", None),
        P("head", None, "seq"),
        P("head", None, None),
        P("head", None, None),
        P("head", None, None),
        P(None, ("head", "seq")),
    )
    return jax.shard_map(
        functools.partial(body, mesh.shape["seq"], mesh.shape["head"]),
        mesh=mesh, in_specs=placed, out_specs=P(None, "seq", "head"), check_vma=False,
    )
```

```python
import functools
import math

import jax
import jax.numpy as jnp
from jax import lax
from jax.experimental import pallas as pl
from jax.experimental.pallas import tpu as pltpu
from jax.sharding import PartitionSpec as P

WINDOW = 256
MOMENTUM = 0.9
LANES = 128
MESH = pl.DeviceIdType.MESH
F32 = jnp.float32
BF16 = jnp.bfloat16


def radices_of(count):
    found = []
    while count > 1:
        if count % 2:
            found.append(count)
        elif len(found) < 2 or count % 4:
            found.append(2)
        else:
            found.append(4)
        count //= found[-1]
    return found


def dot(left, right):
    return jnp.dot(left, right, preferred_element_type=F32)


def dot_t(left, right):
    return lax.dot_general(left, right, (((1,), (1,)), ((), ())), preferred_element_type=F32)


def sigmoid(value):
    return 0.5 * jnp.tanh(0.5 * value) + 0.5


def kernel(
    n_seq, n_head, gather_weight,
    q_hbm, k_hbm, v_hbm, rate_hbm, gate_hbm, down_hbm, up_hbm, ow_hbm,
    out_ref,
    q_ref, k_ref, v_ref, rate_ref, gate_w, down_ref, up_w, ow_ref, down_w,
    mom, start_b, cur, keys_t, target, target_t, k_far, target_far, hid_s, da_s, db_s,
    acc, send_b, recv_b, full_b, sq_out, sq_in, edge_k, edge_v, ow_all, ow_t, mix, win, near,
    load_sem, pair_send, pair_recv, cur_send, cur_recv, sq_send, sq_recv, ar_send, ar_recv, ag_send, ag_recv, halo_send, halo_recv, ow_send, ow_recv, mix_send, mix_recv,
):
    spans, rows, dh = q_ref.shape
    hid = gate_hbm.shape[1]
    ways = radices_of(n_seq)[0]
    hid_part = hid // ways
    cols = hid_part // LANES
    part_rows = cols * dh
    wts = (gate_w, down_w, up_w)
    radices = radices_of(n_seq)
    levels = len(radices)
    me = lax.axis_index("seq")
    head = lax.axis_index("head")
    share = pl.ds(pl.multiple_of(lax.rem(me, ways) * hid_part, hid_part), hid_part)

    loads = {}

    def load(name, source, dest):
        loads[name] = pltpu.make_async_copy(source, dest, load_sem.at[len(loads)])
        loads[name].start()

    load("gate", gate_hbm.at[:, share], gate_w)
    load(("k", 0), k_hbm.at[0], k_ref.at[0])
    load("up", up_hbm.at[:, share], up_w)
    load("rate", rate_hbm, rate_ref)
    load(("v", 0), v_hbm.at[0], v_ref.at[0])
    load("down", down_hbm.at[share], down_ref)
    load("ow", ow_hbm, ow_ref)
    for c in range(1, spans):
        load(("k", c), k_hbm.at[c], k_ref.at[c])
        load(("v", c), v_hbm.at[c], v_ref.at[c])
    load("q", q_hbm, q_ref)

    strides, digits = [], []
    stride = 1
    for radix in radices:
        strides.append(stride)
        digits.append(lax.rem(me // stride, radix))
        stride *= radix

    def peer(level, step):
        radix = radices[level]
        other = lax.rem(digits[level] + step, radix)
        return me + (other - digits[level]) * strides[level], other

    def near_peer(step):
        width = ways * radices[1] if levels > 1 else ways
        spot = lax.rem(me, width)
        return me + lax.rem(spot + step, width) - spot

    near_steps = range(1, ways * (radices[1] if levels > 1 else 1))

    following = lax.rem(me + 1, n_seq)
    before = lax.rem(me + n_seq - 1, n_seq)

    barrier = pltpu.get_barrier_semaphore()
    greeted = 0
    for level in range(levels):
        for step in range(1, radices[level]):
            pl.semaphore_signal(barrier, inc=1, device_id={"seq": peer(level, step)[0]}, device_id_type=MESH)
            greeted += 1
    for step in near_steps:
        pl.semaphore_signal(barrier, inc=1, device_id={"seq": near_peer(step)}, device_id_type=MESH)
        greeted += 1
    for other in (following, before):
        pl.semaphore_signal(barrier, inc=1, device_id={"seq": other}, device_id_type=MESH)
        greeted += 1
    for step in range(1, n_head):
        pl.semaphore_signal(
            barrier, inc=1, device_id={"head": lax.rem(head + step, n_head)}, device_id_type=MESH
        )
        greeted += 1

    def prepare(c):
        rate_row = jnp.broadcast_to(rate_ref[c : c + 1, :], (LANES, rows))
        rate = rate_row.T
        rate = jnp.concatenate([rate] * (dh // LANES), axis=1)
        aim = (-(rate * v_ref[c].astype(F32))).astype(BF16)
        target[c] = aim
        for copy in pair_copies(c, 1):
            copy.start()
        target_t[c, :, :rows] = aim.T
        keys_t[c, :, :rows] = k_ref[c].T

    def pair_copies(c, kind):
        made = []
        for step in range(1, ways):
            source, dest = ((k_hbm, k_far), (target, target_far))[kind]
            made.append(
                pltpu.make_async_remote_copy(
                    src_ref=source.at[c], dst_ref=dest.at[c, step - 1],
                    send_sem=pair_send.at[c, kind, step], recv_sem=pair_recv.at[c, kind, step],
                    device_id={"seq": peer(0, step)[0]}, device_id_type=MESH,
                )
            )
        return made

    def prepare_far(c):
        for kind in range(2):
            for copy in pair_copies(c, kind):
                copy.wait()
        for step in range(1, ways):
            place = slice(step * rows, (step + 1) * rows)
            target_t[c, :, place] = target_far[c, step - 1].T
            keys_t[c, :, place] = k_far[c, step - 1].T

    def gradient(c):
        weights = start_b if c == 0 else cur.at[c - 1, 0]
        piece = min(256, rows)
        for slot in range(ways):
            if c == 0 and slot == 1:
                prepare_far(c)
            for start in range(0, rows, piece):
                part = slice(start, start + piece)
                place = slice(slot * rows + start, slot * rows + start + piece)
                k_part = k_ref[c, part] if slot == 0 else k_far[c, slot - 1, part]
                aim = target[c, part] if slot == 0 else target_far[c, slot - 1, part]
                pre_gate = dot(k_part, weights[0])
                pre_up = dot(k_part, weights[2])
                back = dot(aim, weights[1])
                sig = sigmoid(pre_gate)
                silu = pre_gate * sig
                hid_s[place, :] = (silu * pre_up).astype(BF16)
                da_s[place, :] = (back * pre_up * (sig * (1.0 + pre_gate * (1.0 - sig)))).astype(BF16)
                db_s[place, :] = (back * silu).astype(BF16)
        for p, (left, right) in enumerate(((target_t, hid_s), (keys_t, da_s), (keys_t, db_s))):
            grad = dot(left[c], right[...])
            for cb in range(cols):
                base = p * part_rows + cb * dh
                block = grad[:, cb * LANES : (cb + 1) * LANES]
                acc[base : base + dh, :] = block
                send_b[c, base : base + dh, :] = block.astype(BF16)
            start_stage(c, p, 0)

    def span_of(start, size):
        return pl.ds(pl.multiple_of(start, 16), size)

    def fill(work):
        if work:
            work.pop(0)()

    def owned(unit, level, first):
        start = 0
        for l in range(first, level + 1):
            start = start + digits[l] * (unit * math.prod(radices[l + 1 :]))
        return start

    def gather_copies(buf, offset, unit, level, first, sends, recvs):
        size = unit * math.prod(radices[level + 1 :])
        made = []
        for step in range(1, radices[level]):
            slot = sum(radices[:level]) + step
            block = buf.at[span_of(offset + owned(unit, level, first), size)]
            made.append(
                pltpu.make_async_remote_copy(
                    src_ref=block, dst_ref=block, send_sem=sends.at[slot], recv_sem=recvs.at[slot],
                    device_id={"seq": peer(level, step)[0]}, device_id_type=MESH,
                )
            )
        return made

    unit = part_rows // (n_seq // ways)

    def landing_at(p, level):
        sizes = [unit * math.prod(radices[l + 1 :]) * (radices[l] - 1) for l in range(1, levels)]
        return p * sum(sizes) + sum(sizes[: level - 1])

    def scatter_copies(c, p, level):
        size = unit * math.prod(radices[level + 1 :])
        base = p * part_rows + owned(unit, level - 1, 1)
        made = []
        for step in range(1, radices[level]):
            target_dev, other = peer(level, step)
            slot = sum(radices[:level]) + step
            made.append(
                pltpu.make_async_remote_copy(
                    src_ref=send_b.at[c, span_of(base + other * size, size)],
                    dst_ref=recv_b.at[c, pl.ds(landing_at(p, level) + (step - 1) * size, size)],
                    send_sem=ar_send.at[c, p, slot], recv_sem=ar_recv.at[c, p, slot],
                    device_id={"seq": target_dev}, device_id_type=MESH,
                )
            )
        return made

    halfway = levels - 1
    stages = 2 * halfway

    def stage_copies(c, p, stage):
        if stage < halfway:
            return scatter_copies(c, p, stage + 1)
        return gather_copies(
            full_b.at[c], p * part_rows, unit, stages - stage, 1, ag_send.at[c, p], ag_recv.at[c, p]
        )

    def start_stage(c, p, stage):
        for copy in stage_copies(c, p, stage):
            copy.start()

    def squares_of(value):
        return jnp.sum((value * value).reshape(value.shape[0] // 8, 8, LANES), axis=0)

    def finish_stage(c, p, stage):
        for copy in stage_copies(c, p, stage):
            copy.wait_recv()
        squares = None
        if stage < halfway:
            level = stage + 1
            size = unit * math.prod(radices[level + 1 :])
            place = span_of(p * part_rows + owned(unit, level, 1), size)
            mine = acc[place, :]
            landed = landing_at(p, level)
            for step in range(radices[level] - 1):
                mine += recv_b[c, landed + step * size : landed + (step + 1) * size, :].astype(F32)
            if level < levels - 1:
                acc[place, :] = mine
                send_b[c, place, :] = mine.astype(BF16)
            else:
                full_b[c, place, :] = mine.astype(BF16)
        if stage + 1 < stages:
            start_stage(c, p, stage + 1)
        if stage == halfway - 1:
            squares = squares_of(mine)
        return squares

    def norm_copies(c, index):
        level = levels - 1 - index
        made = []
        for step in range(1, radices[level]) if level > 1 else near_steps:
            other = peer(level, step)[0] if level > 1 else near_peer(step)
            made.append(
                pltpu.make_async_remote_copy(
                    src_ref=sq_out.at[c, index], dst_ref=sq_in.at[c, index, step],
                    send_sem=sq_send.at[c, index, step], recv_sem=sq_recv.at[c, index, step],
                    device_id={"seq": other}, device_id_type=MESH,
                )
            )
        return made

    def norm_start(c, index, squares):
        sq_out[c, index] = squares
        for copy in norm_copies(c, index):
            copy.start()

    def norm_finish(c, index):
        squares = sq_out[c, index]
        count = 1
        for copy in norm_copies(c, index):
            copy.wait()
            squares = squares + sq_in[c, index, count]
            count += 1
        return squares

    def all_reduce(c, work):
        squares = None
        for key in range(stages + 2):
            fill(work)
            for p in reversed(range(3)):
                stage = key - p
                if 0 <= stage < stages:
                    term = finish_stage(c, p, stage)
                    if term is not None:
                        squares = term if squares is None else squares + term
            if key >= halfway + 1:
                index = key - halfway - 1
                if index > 0:
                    squares = norm_finish(c, index - 1)
                if index < halfway:
                    norm_start(c, index, squares)
        while work:
            fill(work)
        return squares

    def settle(c):
        for p in range(3):
            for stage in range(stages):
                for copy in stage_copies(c, p, stage):
                    copy.wait_send()

    def cur_copies(c):
        made = []
        for step in range(1, ways):
            made.append(
                pltpu.make_async_remote_copy(
                    src_ref=cur.at[c, 0], dst_ref=cur.at[c, step],
                    send_sem=cur_send.at[c, step], recv_sem=cur_recv.at[c, step],
                    device_id={"seq": peer(0, step)[0]}, device_id_type=MESH,
                )
            )
        return made

    def update(c, squares):
        whole = jnp.sum(jnp.sum(squares, axis=1, keepdims=True), axis=0, keepdims=True)
        factor = jnp.minimum(1.0, 0.6 * math.sqrt(hid) / jnp.sqrt(whole + 1e-6))
        for p, m in ((1, 0), (2, 2), (0, 1)):
            for cb in range(cols):
                base = p * part_rows + cb * dh
                lanes = slice(cb * LANES, (cb + 1) * LANES)
                change = factor * full_b[c, base : base + dh, :].astype(F32)
                if c > 0:
                    change = MOMENTUM * mom[m, :, lanes] + change
                fresh = wts[m][:, lanes] - change
                if c < spans - 1:
                    mom[m, :, lanes] = change
                    wts[m][:, lanes] = fresh
                cur[c, 0, m, :, lanes] = fresh.astype(BF16)
        for copy in cur_copies(c):
            copy.start()

    row_ids = lax.broadcasted_iota(jnp.int32, (WINDOW, WINDOW), 0)
    col_ids = lax.broadcasted_iota(jnp.int32, (WINDOW, WINDOW), 1)
    scale = 1.0 / math.sqrt(dh)

    def attend(c, j):
        start = j * WINDOW
        here = slice(start, start + WINDOW)
        left_ok = col_ids > row_ids
        if j == 0:
            first = me == 0
            span = jnp.where(first, (c + spans - 1) % spans, c)
            left_k, left_v = edge_k[span], edge_v[span]
            if c == 0:
                left_ok = left_ok & jnp.logical_not(first)
        else:
            earlier = slice(start - WINDOW, start)
            left_k, left_v = k_ref[c, earlier], v_ref[c, earlier]
        query = q_ref[c, here]
        left = jnp.where(left_ok, dot_t(query, left_k) * scale, -1e30)
        right = jnp.where(col_ids <= row_ids, dot_t(query, k_ref[c, here]) * scale, -1e30)
        top = jnp.maximum(jnp.max(left, axis=1, keepdims=True), jnp.max(right, axis=1, keepdims=True))
        left = jnp.exp(left - top)
        right = jnp.exp(right - top)
        share = 1.0 / (jnp.sum(left, axis=1, keepdims=True) + jnp.sum(right, axis=1, keepdims=True))
        win[c, here] = dot((left * share).astype(BF16), left_v) + dot(
            (right * share).astype(BF16), v_ref[c, here]
        )

    half = WINDOW

    def mix_copies(c, j):
        made = []
        for step in range(1, n_head):
            block = mix.at[head, c, pl.ds(j * half, half)]
            made.append(
                pltpu.make_async_remote_copy(
                    src_ref=block, dst_ref=block,
                    send_sem=mix_send.at[c, j, step], recv_sem=mix_recv.at[c, j, step],
                    device_id={"head": lax.rem(head + step, n_head)}, device_id_type=MESH,
                )
            )
        return made

    def fast_part(c, j, slot):
        query = q_ref[c, j * half : (j + 1) * half]
        pre_gate = dot(query, cur[c, slot, 0])
        hidden = (pre_gate * sigmoid(pre_gate) * dot(query, cur[c, slot, 2])).astype(BF16)
        return dot_t(hidden, cur[c, slot, 1])

    def apply_near(c, j):
        near[c, j * half : (j + 1) * half] = fast_part(c, j, 0)

    def apply_far(c, j):
        part = slice(j * half, (j + 1) * half)
        if j == 0:
            for copy in cur_copies(c):
                copy.wait()
        fast = near[c, part]
        for slot in range(1, ways):
            fast = fast + fast_part(c, j, slot)
        norm = fast * lax.rsqrt(jnp.mean(fast * fast, axis=-1, keepdims=True) + 1e-5)
        mix[head, c, part] = (norm + win[c, part]).astype(BF16)
        for copy in mix_copies(c, j):
            copy.start()

    def apply(c, j):
        apply_near(c, j)
        apply_far(c, j)

    def project(c, j):
        part = slice(j * half, (j + 1) * half)
        for copy in mix_copies(c, j):
            copy.wait()
        result = None
        for h in range(n_head):
            term = dot_t(mix[h, c, part], ow_t[:, h * dh : (h + 1) * dh])
            result = term if result is None else result + term
        out_ref[c, part] = result.astype(BF16)

    halo = []
    for index, (source, dest) in enumerate(((k_hbm, edge_k), (v_hbm, edge_v))):
        for c in range(spans):
            halo.append(
                pltpu.make_async_remote_copy(
                    src_ref=source.at[c, pl.ds(rows - WINDOW, WINDOW)], dst_ref=dest.at[c],
                    send_sem=halo_send.at[index, c], recv_sem=halo_recv.at[index, c],
                    device_id={"seq": following}, device_id_type=MESH,
                )
            )

    shard = ow_ref.shape[0]

    def weight_copies(level):
        return gather_copies(ow_all, 0, shard, level, 0, ow_send, ow_recv)

    def weight_next(level):
        if level < levels - 1:
            for copy in weight_copies(level + 1):
                copy.wait()
        for copy in weight_copies(level):
            copy.start()

    def weight_end():
        for copy in weight_copies(0):
            copy.wait()
        for s in range(n_seq):
            place, rest = 0, s
            for radix in radices:
                place = place * radix + rest % radix
                rest //= radix
            ow_t[s * shard : (s + 1) * shard, :] = ow_all[place * shard : (place + 1) * shard, :]

    tiles = rows // WINDOW
    pl.semaphore_wait(barrier, greeted)
    for c in range(spans):
        for copy in pair_copies(c, 0):
            copy.start()
        if c == 0:
            for copy in halo:
                copy.start()
    loads["rate"].wait()
    loads[("k", 0)].wait()
    loads[("v", 0)].wait()
    prepare(0)
    loads["gate"].wait()
    start_b[0] = gate_w[...].astype(BF16)
    loads["up"].wait()
    start_b[2] = up_w[...].astype(BF16)
    loads["down"].wait()
    down_w[...] = down_ref[...].T
    start_b[1] = down_w[...].astype(BF16)
    loads["ow"].wait()
    if gather_weight:
        ow_all[span_of(owned(shard, levels - 1, 0), shard), :] = ow_ref[...]
        weight_next(levels - 1)
    else:
        ow_t[...] = ow_ref[...]
    gradient(0)
    loads["q"].wait()
    for c in range(1, spans):
        loads[("k", c)].wait()
        loads[("v", c)].wait()
    for c in range(spans):
        work = []
        if c + 1 < spans:
            work.append(functools.partial(prepare, c + 1))
        if c == 0:
            work += [functools.partial(attend, s, j) for s in range(spans) for j in range(1, tiles)]

            def edges():
                for copy in halo:
                    copy.wait()
                attend(0, 0)

            work.append(edges)
            work += [functools.partial(attend, s, 0) for s in range(1, spans)]
        if c + 1 < spans:
            work.append(functools.partial(prepare_far, c + 1))
        if c > 0:
            work += [functools.partial(apply, c - 1, j) for j in range(tiles)]
        if c == spans - 1:
            if gather_weight:
                first = levels - 2 if c > 0 else levels - 1
                work += [functools.partial(weight_next, level) for level in reversed(range(first))]
                work.append(weight_end)
            work += [functools.partial(project, s, j) for s in range(c) for j in range(tiles)]
        update(c, all_reduce(c, work))
        if c + 1 < spans:
            if c + 1 == spans - 1 and gather_weight and levels > 1:
                weight_next(levels - 2)
            gradient(c + 1)
    for j in range(tiles):
        apply_near(spans - 1, j)
    for j in range(tiles):
        apply_far(spans - 1, j)
    for c in range(spans):
        settle(c)
    for j in range(tiles):
        project(spans - 1, j)


def body(n_seq, n_head, queries, key_rows, values, learn_rates, fast_gate, fast_down, fast_up, output_weight):
    spans, rows, _, dh = queries.shape
    hid = fast_gate.shape[2]
    features, shard = output_weight.shape
    gather_weight = shard % 16 == 0
    if gather_weight:
        weight = output_weight.T
    else:
        weight = lax.all_gather(output_weight, "seq", axis=1, tiled=True).T
    out_cols = shard * n_seq
    radices = radices_of(n_seq)
    ways = radices[0]
    hid_part = hid // ways
    cols = hid_part // LANES
    total = 3 * cols * dh
    landing, size = 0, total
    for radix in radices[1:]:
        size //= radix
        landing += (radix - 1) * size
    near_count = ways * max(radices[1:2] + [1])
    widest = max([near_count] + radices)
    norms = max(len(radices) - 1, 1)
    slots = sum(radices) + 1
    tiles = rows // WINDOW
    dma = pltpu.SemaphoreType.DMA
    vmem = pltpu.VMEM
    return pl.pallas_call(
        functools.partial(kernel, n_seq, n_head, gather_weight),
        out_shape=jax.ShapeDtypeStruct((spans, rows, out_cols), BF16),
        in_specs=[pl.BlockSpec(memory_space=pltpu.HBM)] * 8,
        out_specs=pl.BlockSpec(memory_space=pltpu.VMEM),
        scratch_shapes=[
            vmem((spans, rows, dh), BF16),
            vmem((spans, rows, dh), BF16),
            vmem((spans, rows, dh), BF16),
            vmem((spans, rows), F32),
            vmem((dh, hid_part), F32),
            vmem((hid_part, dh), F32),
            vmem((dh, hid_part), F32),
            vmem(weight.shape, BF16),
            vmem((dh, hid_part), F32),
            vmem((3, dh, hid_part), F32),
            vmem((3, dh, hid_part), BF16),
            vmem((spans, ways, 3, dh, hid_part), BF16),
            vmem((spans, dh, ways * rows), BF16),
            vmem((spans, rows, dh), BF16),
            vmem((spans, dh, ways * rows), BF16),
            vmem((spans, ways - 1, rows, dh), BF16),
            vmem((spans, ways - 1, rows, dh), BF16),
            vmem((ways * rows, hid_part), BF16),
            vmem((ways * rows, hid_part), BF16),
            vmem((ways * rows, hid_part), BF16),
            vmem((total, LANES), F32),
            vmem((spans, total, LANES), BF16),
            vmem((spans, landing, LANES), BF16),
            vmem((spans, total, LANES), BF16),
            vmem((spans, norms, 8, LANES), F32),
            vmem((spans, norms, widest, 8, LANES), F32),
            vmem((spans, WINDOW, dh), BF16),
            vmem((spans, WINDOW, dh), BF16),
            vmem((out_cols, features), BF16),
            vmem((out_cols, features), BF16),
            vmem((n_head, spans, rows, dh), BF16),
            vmem((spans, rows, dh), F32),
            vmem((spans, rows, dh), F32),
            dma((6 + 2 * spans,)),
            dma((spans, 2, ways)),
            dma((spans, 2, ways)),
            dma((spans, ways)),
            dma((spans, ways)),
            dma((spans, norms, widest)),
            dma((spans, norms, widest)),
            dma((spans, 3, slots)),
            dma((spans, 3, slots)),
            dma((spans, 3, slots)),
            dma((spans, 3, slots)),
            dma((2, spans)),
            dma((2, spans)),
            dma((slots,)),
            dma((slots,)),
            dma((spans, tiles, n_head)),
            dma((spans, tiles, n_head)),
        ],
        compiler_params=pltpu.CompilerParams(
            collective_id=0, has_side_effects=True, vmem_limit_bytes=60 * 1024 * 1024
        ),
    )(
        queries[:, :, 0, :], key_rows[:, :, 0, :], values[:, :, 0, :], learn_rates[0],
        fast_gate[0], fast_down[0], fast_up[0], weight,
    )


def solution(mesh):
    placed = (
        P(None, "seq", "head", None),
        P(None, "seq", "head", None),
        P(None, "seq", "head", None),
        P("head", None, "seq"),
        P("head", None, None),
        P("head", None, None),
        P("head", None, None),
        P(None, ("head", "seq")),
    )
    return jax.shard_map(
        functools.partial(body, mesh.shape["seq"], mesh.shape["head"]),
        mesh=mesh, in_specs=placed, out_specs=P(None, "seq", "head"), check_vma=False,
    )
```

```python
import functools
import math

import jax
import jax.numpy as jnp
from jax import lax
from jax.experimental import pallas as pl
from jax.experimental.pallas import tpu as pltpu
from jax.sharding import PartitionSpec as P

WINDOW = 256
MOMENTUM = 0.9
LANES = 128
CHUNK = 16
MESH = pl.DeviceIdType.MESH
F32 = jnp.float32
BF16 = jnp.bfloat16


def radices_of(count):
    found = []
    while count > 1:
        if count % 2:
            found.append(count)
        elif len(found) < 2 or count % 4:
            found.append(2)
        else:
            found.append(4)
        count //= found[-1]
    return found


def dot(left, right):
    return jnp.dot(left, right, preferred_element_type=F32)


def dot_t(left, right):
    return lax.dot_general(left, right, (((1,), (1,)), ((), ())), preferred_element_type=F32)


def sigmoid(value):
    return 0.5 * jnp.tanh(0.5 * value) + 0.5


def kernel(
    n_seq, n_head, gather_weight,
    q_hbm, k_hbm, v_hbm, rate_hbm, gate_hbm, down_hbm, up_hbm, ow_hbm,
    out_ref,
    q_ref, k_ref, v_ref, rate_ref, gate_w, down_ref, up_w, ow_ref, down_w,
    mom, gate_b, up_b, down_tb, keys_t, target, target_t, hid_s, da_s, db_s,
    gate_f, up_f, back_f, score_f, prob_s, hidden_s, fast_f,
    acc, send_b, recv_b, full_b, edge_k, edge_v, ow_all, ow_t, mix, win,
    load_sem, ar_send, ar_recv, ag_send, ag_recv, halo_send, halo_recv, ow_send, ow_recv, mix_send, mix_recv,
):
    spans, rows, dh = q_ref.shape
    hid = gate_w.shape[1]
    cols = hid // LANES
    part_rows = cols * dh
    wts = (gate_w, down_w, up_w)
    current = (gate_b, down_tb, up_b)
    radices = radices_of(n_seq)
    levels = len(radices)
    me = lax.axis_index("seq")
    head = lax.axis_index("head")

    loads = {}

    def load(name, source, dest):
        loads[name] = pltpu.make_async_copy(source, dest, load_sem.at[len(loads)])
        loads[name].start()

    load("gate", gate_hbm, gate_w)
    load(("k", 0), k_hbm.at[0], k_ref.at[0])
    load("up", up_hbm, up_w)
    load("rate", rate_hbm, rate_ref)
    load(("v", 0), v_hbm.at[0], v_ref.at[0])
    load("down", down_hbm, down_ref)
    load("ow", ow_hbm, ow_ref)
    for c in range(1, spans):
        load(("k", c), k_hbm.at[c], k_ref.at[c])
        load(("v", c), v_hbm.at[c], v_ref.at[c])
    load("q", q_hbm, q_ref)

    strides, digits = [], []
    stride = 1
    for radix in radices:
        strides.append(stride)
        digits.append(lax.rem(me // stride, radix))
        stride *= radix

    def peer(level, step):
        radix = radices[level]
        other = lax.rem(digits[level] + step, radix)
        return me + (other - digits[level]) * strides[level], other

    following = lax.rem(me + 1, n_seq)
    before = lax.rem(me + n_seq - 1, n_seq)

    barrier = pltpu.get_barrier_semaphore()
    greeted = 0
    for level in range(levels):
        for step in range(1, radices[level]):
            pl.semaphore_signal(barrier, inc=1, device_id={"seq": peer(level, step)[0]}, device_id_type=MESH)
            greeted += 1
    for other in (following, before):
        pl.semaphore_signal(barrier, inc=1, device_id={"seq": other}, device_id_type=MESH)
        greeted += 1
    for step in range(1, n_head):
        pl.semaphore_signal(
            barrier, inc=1, device_id={"head": lax.rem(head + step, n_head)}, device_id_type=MESH
        )
        greeted += 1

    def prepare(c):
        rate_row = jnp.broadcast_to(rate_ref[c : c + 1, :], (LANES, rows))
        rate = rate_row.T
        rate = jnp.concatenate([rate] * (dh // LANES), axis=1)
        aim = (-(rate * v_ref[c].astype(F32))).astype(BF16)
        target[...] = aim
        target_t[...] = aim.T
        keys_t[...] = k_ref[c].T

    def gradient(c):
        piece = min(256, rows)
        for start in range(0, rows, piece):
            part = slice(start, start + piece)
            k_part = k_ref[c, part]
            gate_f[part, :] = dot(k_part, gate_b[...])
            up_f[part, :] = dot(k_part, up_b[...])
            back_f[part, :] = dot(target[part, :], down_tb[...])
            for r in range(start, start + piece, CHUNK):
                at = slice(r, r + CHUNK)
                pre_gate, pre_up, back = gate_f[at, :], up_f[at, :], back_f[at, :]
                sig = sigmoid(pre_gate)
                silu = pre_gate * sig
                hid_s[at, :] = (silu * pre_up).astype(BF16)
                da_s[at, :] = (back * pre_up * (sig * (1.0 + pre_gate * (1.0 - sig)))).astype(BF16)
                db_s[at, :] = (back * silu).astype(BF16)
        for p, (left, right) in enumerate(((target_t, hid_s), (keys_t, da_s), (keys_t, db_s))):
            grad = dot(left[...], right[...])
            for cb in range(cols):
                base = p * part_rows + cb * dh
                block = grad[:, cb * LANES : (cb + 1) * LANES]
                acc[base : base + dh, :] = block
                send_b[c, base : base + dh, :] = block.astype(BF16)
            start_stage(c, p, 0)

    def span_of(start, size):
        return pl.ds(pl.multiple_of(start, 16), size)

    def fill(work):
        if work:
            work.pop(0)()

    def owned(unit, level):
        start = 0
        for l in range(level + 1):
            start = start + digits[l] * (unit * math.prod(radices[l + 1 :]))
        return start

    def gather_copies(buf, offset, unit, level, sends, recvs):
        size = unit * math.prod(radices[level + 1 :])
        made = []
        for step in range(1, radices[level]):
            slot = sum(radices[:level]) + step
            block = buf.at[span_of(offset + owned(unit, level), size)]
            made.append(
                pltpu.make_async_remote_copy(
                    src_ref=block, dst_ref=block, send_sem=sends.at[slot], recv_sem=recvs.at[slot],
                    device_id={"seq": peer(level, step)[0]}, device_id_type=MESH,
                )
            )
        return made

    unit = part_rows // n_seq

    def scatter_copies(c, p, level):
        size = unit * math.prod(radices[level + 1 :])
        base = p * part_rows + (owned(unit, level - 1) if level else 0)
        made = []
        for step in range(1, radices[level]):
            target_dev, other = peer(level, step)
            slot = sum(radices[:level]) + step
            made.append(
                pltpu.make_async_remote_copy(
                    src_ref=send_b.at[c, span_of(base + other * size, size)],
                    dst_ref=recv_b.at[c, pl.ds(landing_at(p, level) + (step - 1) * size, size)],
                    send_sem=ar_send.at[c, p, slot], recv_sem=ar_recv.at[c, p, slot],
                    device_id={"seq": target_dev}, device_id_type=MESH,
                )
            )
        return made

    def landing_at(p, level):
        sizes = [unit * math.prod(radices[l + 1 :]) * (radices[l] - 1) for l in range(levels)]
        return p * sum(sizes) + sum(sizes[:level])

    stages = 2 * levels

    def stage_copies(c, p, stage):
        if stage < levels:
            return scatter_copies(c, p, stage)
        return gather_copies(
            full_b.at[c], p * part_rows, unit, stages - 1 - stage, ag_send.at[c, p], ag_recv.at[c, p]
        )

    def start_stage(c, p, stage):
        for copy in stage_copies(c, p, stage):
            copy.start()

    def finish_stage(c, p, stage):
        for copy in stage_copies(c, p, stage):
            copy.wait_recv()
        if stage < levels:
            size = unit * math.prod(radices[stage + 1 :])
            place = span_of(p * part_rows + owned(unit, stage), size)
            mine = acc[place, :]
            landed = landing_at(p, stage)
            for step in range(radices[stage] - 1):
                mine += recv_b[c, landed + step * size : landed + (step + 1) * size, :].astype(F32)
            if stage < levels - 1:
                acc[place, :] = mine
                send_b[c, place, :] = mine.astype(BF16)
            else:
                full_b[c, place, :] = mine.astype(BF16)
        if stage + 1 < stages:
            start_stage(c, p, stage + 1)

    def all_reduce(c, work):
        squares = jnp.zeros((8, LANES), F32)
        for p in range(3):
            finish_stage(c, p, 0)
        for key in range(1, stages + 2):
            fill(work)
            for p in reversed(range(3)):
                stage = key - p
                if 1 <= stage < stages:
                    finish_stage(c, p, stage)
                    if stage == stages - 1:
                        for cb in range(cols):
                            base = p * part_rows + cb * dh
                            block = full_b[c, base : base + dh, :].astype(F32)
                            squares += jnp.sum((block * block).reshape(dh // 8, 8, LANES), axis=0)
        while work:
            fill(work)
        for p in range(3):
            for stage in range(stages):
                for copy in stage_copies(c, p, stage):
                    copy.wait_send()
        return squares

    def update(c, squares):
        whole = jnp.sum(jnp.sum(squares, axis=1, keepdims=True), axis=0, keepdims=True)
        factor = jnp.minimum(1.0, 0.6 * math.sqrt(hid) / jnp.sqrt(whole + 1e-6))
        for p, m in ((1, 0), (2, 2), (0, 1)):
            for cb in range(cols):
                base = p * part_rows + cb * dh
                lanes = slice(cb * LANES, (cb + 1) * LANES)
                for r in range(0, dh, 64):
                    at = slice(r, r + 64)
                    change = factor * full_b[c, base + r : base + r + 64, :].astype(F32)
                    if c > 0:
                        change = MOMENTUM * mom[m, at, lanes] + change
                    fresh = wts[m][at, lanes] - change
                    if c < spans - 1:
                        mom[m, at, lanes] = change
                        wts[m][at, lanes] = fresh
                    current[m][at, lanes] = fresh.astype(BF16)

    scale = 1.0 / math.sqrt(dh)

    def attend(c, j):
        start = j * WINDOW
        here = slice(start, start + WINDOW)
        if j == 0:
            first = me == 0
            span = jnp.where(first, (c + spans - 1) % spans, c)
            left_k, left_v = edge_k[span], edge_v[span]
        else:
            earlier = slice(start - WINDOW, start)
            left_k, left_v = k_ref[c, earlier], v_ref[c, earlier]
        query = q_ref[c, here]
        score_f[:, :WINDOW] = dot_t(query, left_k)
        score_f[:, WINDOW:] = dot_t(query, k_ref[c, here])
        for r in range(0, WINDOW, CHUNK):
            at = slice(r, r + CHUNK)
            row_ids = lax.broadcasted_iota(jnp.int32, (CHUNK, 2 * WINDOW), 0) + r
            col_ids = lax.broadcasted_iota(jnp.int32, (CHUNK, 2 * WINDOW), 1)
            lowest = row_ids
            if j == 0 and c == 0:
                lowest = jnp.maximum(lowest, jnp.where(me == 0, WINDOW - 1, 0))
            ok = (col_ids > lowest) & (col_ids <= row_ids + WINDOW)
            scores = jnp.where(ok, score_f[at, :] * scale, -1e30)
            scores = jnp.exp(scores - jnp.max(scores, axis=1, keepdims=True))
            share = 1.0 / jnp.sum(scores, axis=1, keepdims=True)
            prob_s[at, :] = (scores * share).astype(BF16)
        win[c, here] = dot(prob_s[:, :WINDOW], left_v) + dot(prob_s[:, WINDOW:], v_ref[c, here])

    half = WINDOW

    def mix_copies(c, j):
        made = []
        for step in range(1, n_head):
            block = mix.at[head, c, pl.ds(j * half, half)]
            made.append(
                pltpu.make_async_remote_copy(
                    src_ref=block, dst_ref=block,
                    send_sem=mix_send.at[c, j, step], recv_sem=mix_recv.at[c, j, step],
                    device_id={"head": lax.rem(head + step, n_head)}, device_id_type=MESH,
                )
            )
        return made

    def apply(c, j):
        part = slice(j * half, (j + 1) * half)
        query = q_ref[c, part]
        gate_f[part, :] = dot(query, gate_b[...])
        up_f[part, :] = dot(query, up_b[...])
        for r in range(0, half, CHUNK):
            at = slice(j * half + r, j * half + r + CHUNK)
            pre_gate = gate_f[at, :]
            hidden_s[r : r + CHUNK, :] = (pre_gate * sigmoid(pre_gate) * up_f[at, :]).astype(BF16)
        fast_f[...] = dot_t(hidden_s[...], down_tb[...])
        for r in range(0, half, CHUNK):
            at = slice(j * half + r, j * half + r + CHUNK)
            fast = fast_f[r : r + CHUNK, :]
            norm = fast * lax.rsqrt(jnp.mean(fast * fast, axis=-1, keepdims=True) + 1e-5)
            mix[head, c, at] = (norm + win[c, at]).astype(BF16)
        for copy in mix_copies(c, j):
            copy.start()

    def project(c, j):
        part = slice(j * half, (j + 1) * half)
        for copy in mix_copies(c, j):
            copy.wait()
        result = None
        for h in range(n_head):
            term = dot_t(mix[h, c, part], ow_t[:, h * dh : (h + 1) * dh])
            result = term if result is None else result + term
        out_ref[c, part] = result.astype(BF16)

    halo = []
    for index, (source, dest) in enumerate(((k_hbm, edge_k), (v_hbm, edge_v))):
        for c in range(spans):
            halo.append(
                pltpu.make_async_remote_copy(
                    src_ref=source.at[c, pl.ds(rows - WINDOW, WINDOW)], dst_ref=dest.at[c],
                    send_sem=halo_send.at[index, c], recv_sem=halo_recv.at[index, c],
                    device_id={"seq": following}, device_id_type=MESH,
                )
            )

    shard = ow_ref.shape[0]

    def weight_copies(level):
        return gather_copies(ow_all, 0, shard, level, ow_send, ow_recv)

    def weight_next(level):
        if level < levels - 1:
            for copy in weight_copies(level + 1):
                copy.wait()
        for copy in weight_copies(level):
            copy.start()

    def weight_end():
        for copy in weight_copies(0):
            copy.wait()
        for s in range(n_seq):
            place, rest = 0, s
            for radix in radices:
                place = place * radix + rest % radix
                rest //= radix
            ow_t[s * shard : (s + 1) * shard, :] = ow_all[place * shard : (place + 1) * shard, :]

    tiles = rows // WINDOW
    pl.semaphore_wait(barrier, greeted)
    for copy in halo:
        copy.start()
    loads["gate"].wait()
    gate_b[...] = gate_w[...].astype(BF16)
    loads["up"].wait()
    up_b[...] = up_w[...].astype(BF16)
    loads["down"].wait()
    down_w[...] = down_ref[...].T
    down_tb[...] = down_w[...].astype(BF16)
    loads["rate"].wait()
    loads[("k", 0)].wait()
    loads[("v", 0)].wait()
    prepare(0)
    loads["ow"].wait()
    if gather_weight:
        ow_all[span_of(owned(shard, levels - 1), shard), :] = ow_ref[...]
        weight_next(levels - 1)
    else:
        ow_t[...] = ow_ref[...]
    gradient(0)
    loads["q"].wait()
    for c in range(1, spans):
        loads[("k", c)].wait()
        loads[("v", c)].wait()
    for c in range(spans):
        work = []
        if c + 1 < spans:
            work.append(functools.partial(prepare, c + 1))
        if c == 0:
            work += [functools.partial(attend, s, j) for s in range(spans) for j in range(1, tiles)]

            def edges():
                for copy in halo:
                    copy.wait()
                attend(0, 0)

            work.append(edges)
            work += [functools.partial(attend, s, 0) for s in range(1, spans)]
        if c > 0:
            work += [functools.partial(apply, c - 1, j) for j in range(tiles)]
        if c == spans - 1:
            if gather_weight:
                first = levels - 2 if c > 0 else levels - 1
                work += [functools.partial(weight_next, level) for level in reversed(range(first))]
                work.append(weight_end)
            work += [functools.partial(project, s, j) for s in range(c) for j in range(tiles)]
        update(c, all_reduce(c, work))
        if c + 1 < spans:
            if c + 1 == spans - 1 and gather_weight and levels > 1:
                weight_next(levels - 2)
            gradient(c + 1)
    for j in range(tiles):
        apply(spans - 1, j)
    for j in range(tiles):
        project(spans - 1, j)


def body(n_seq, n_head, queries, key_rows, values, learn_rates, fast_gate, fast_down, fast_up, output_weight):
    spans, rows, _, dh = queries.shape
    hid = fast_gate.shape[2]
    features, shard = output_weight.shape
    gather_weight = shard % 16 == 0
    if gather_weight:
        weight = output_weight.T
    else:
        weight = lax.all_gather(output_weight, "seq", axis=1, tiled=True).T
    out_cols = shard * n_seq
    cols = hid // LANES
    total = 3 * cols * dh
    radices = radices_of(n_seq)
    landing, size = 0, total
    for radix in radices:
        size //= radix
        landing += (radix - 1) * size
    slots = sum(radices) + 1
    tiles = rows // WINDOW
    dma = pltpu.SemaphoreType.DMA
    vmem = pltpu.VMEM
    return pl.pallas_call(
        functools.partial(kernel, n_seq, n_head, gather_weight),
        out_shape=jax.ShapeDtypeStruct((spans, rows, out_cols), BF16),
        in_specs=[pl.BlockSpec(memory_space=pltpu.HBM)] * 8,
        out_specs=pl.BlockSpec(memory_space=pltpu.VMEM),
        scratch_shapes=[
            vmem((spans, rows, dh), BF16),
            vmem((spans, rows, dh), BF16),
            vmem((spans, rows, dh), BF16),
            vmem((spans, rows), F32),
            vmem((dh, hid), F32),
            vmem((hid, dh), F32),
            vmem((dh, hid), F32),
            vmem(weight.shape, BF16),
            vmem((dh, hid), F32),
            vmem((3, dh, hid), F32),
            vmem((dh, hid), BF16),
            vmem((dh, hid), BF16),
            vmem((dh, hid), BF16),
            vmem((dh, rows), BF16),
            vmem((rows, dh), BF16),
            vmem((dh, rows), BF16),
            vmem((rows, hid), BF16),
            vmem((rows, hid), BF16),
            vmem((rows, hid), BF16),
            vmem((rows, hid), F32),
            vmem((rows, hid), F32),
            vmem((rows, hid), F32),
            vmem((WINDOW, 2 * WINDOW), F32),
            vmem((WINDOW, 2 * WINDOW), BF16),
            vmem((WINDOW, hid), BF16),
            vmem((WINDOW, dh), F32),
            vmem((total, LANES), F32),
            vmem((spans, total, LANES), BF16),
            vmem((spans, landing, LANES), BF16),
            vmem((spans, total, LANES), BF16),
            vmem((spans, WINDOW, dh), BF16),
            vmem((spans, WINDOW, dh), BF16),
            vmem((out_cols, features), BF16),
            vmem((out_cols, features), BF16),
            vmem((n_head, spans, rows, dh), BF16),
            vmem((spans, rows, dh), F32),
            dma((6 + 2 * spans,)),
            dma((spans, 3, slots)),
            dma((spans, 3, slots)),
            dma((spans, 3, slots)),
            dma((spans, 3, slots)),
            dma((2, spans)),
            dma((2, spans)),
            dma((slots,)),
            dma((slots,)),
            dma((spans, tiles, n_head)),
            dma((spans, tiles, n_head)),
        ],
        compiler_params=pltpu.CompilerParams(
            collective_id=0, has_side_effects=True, vmem_limit_bytes=60 * 1024 * 1024
        ),
    )(
        queries[:, :, 0, :], key_rows[:, :, 0, :], values[:, :, 0, :], learn_rates[0],
        fast_gate[0], fast_down[0], fast_up[0], weight,
    )


def solution(mesh):
    placed = (
        P(None, "seq", "head", None),
        P(None, "seq", "head", None),
        P(None, "seq", "head", None),
        P("head", None, "seq"),
        P("head", None, None),
        P("head", None, None),
        P("head", None, None),
        P(None, ("head", "seq")),
    )
    return jax.shard_map(
        functools.partial(body, mesh.shape["seq"], mesh.shape["head"]),
        mesh=mesh, in_specs=placed, out_specs=P(None, "seq", "head"), check_vma=False,
    )
```

```python
import functools
import math

import jax
import jax.numpy as jnp
from jax import lax
from jax.experimental import pallas as pl
from jax.experimental.pallas import tpu as pltpu
from jax.sharding import PartitionSpec as P

WINDOW = 256
MOMENTUM = 0.9
LANES = 128
CHUNK = 16
PARTS = 2
MESH = pl.DeviceIdType.MESH
F32 = jnp.float32
BF16 = jnp.bfloat16


def radices_of(count):
    found = []
    while count > 1:
        if count % 2:
            found.append(count)
        elif len(found) < 2 or count % 4:
            found.append(2)
        else:
            found.append(4)
        count //= found[-1]
    return found


def parts_of(rows, holders):
    return PARTS if rows % (PARTS * holders * 16) == 0 else 1


def dot(left, right):
    return jnp.dot(left, right, preferred_element_type=F32)


def dot_t(left, right):
    return lax.dot_general(left, right, (((1,), (1,)), ((), ())), preferred_element_type=F32)


def sigmoid(value):
    return 0.5 * jnp.tanh(0.5 * value) + 0.5


def kernel(
    n_seq, n_head, gather_weight,
    q_hbm, k_hbm, v_hbm, rate_hbm, gate_hbm, down_hbm, up_hbm, ow_hbm,
    out_ref,
    q_ref, k_ref, v_ref, rate_ref, gate_w, down_ref, up_w, ow_ref, down_w,
    mom, start_b, cur, keys_t, target, target_t, k_far, target_far, hid_s, da_s, db_s,
    gate_f, up_f, back_f, score_f, prob_s, hidden_s, fast_f,
    acc, send_b, recv_b, full_b, sq_out, sq_in, edge_k, edge_v, ow_all, ow_t, mix, win, near,
    load_sem, pair_send, pair_recv, cur_send, cur_recv, sq_send, sq_recv, ar_send, ar_recv, ag_send, ag_recv, halo_send, halo_recv, ow_send, ow_recv, mix_send, mix_recv,
):
    spans, rows, dh = q_ref.shape
    hid = gate_hbm.shape[1]
    ways = radices_of(n_seq)[0]
    hid_part = hid // ways
    cols = hid_part // LANES
    matrix_rows = cols * dh
    parts = parts_of(3 * matrix_rows, n_seq // ways)
    part_rows = 3 * matrix_rows // parts
    wts = (gate_w, down_w, up_w)
    radices = radices_of(n_seq)
    levels = len(radices)
    me = lax.axis_index("seq")
    head = lax.axis_index("head")
    share = pl.ds(pl.multiple_of(lax.rem(me, ways) * hid_part, hid_part), hid_part)

    loads = {}

    def load(name, source, dest):
        loads[name] = pltpu.make_async_copy(source, dest, load_sem.at[len(loads)])
        loads[name].start()

    load("gate", gate_hbm.at[:, share], gate_w)
    load(("k", 0), k_hbm.at[0], k_ref.at[0])
    load("up", up_hbm.at[:, share], up_w)
    load("rate", rate_hbm, rate_ref)
    load(("v", 0), v_hbm.at[0], v_ref.at[0])
    load("down", down_hbm.at[share], down_ref)
    load("ow", ow_hbm, ow_ref)
    for c in range(1, spans):
        load(("k", c), k_hbm.at[c], k_ref.at[c])
        load(("v", c), v_hbm.at[c], v_ref.at[c])
    load("q", q_hbm, q_ref)

    strides, digits = [], []
    stride = 1
    for radix in radices:
        strides.append(stride)
        digits.append(lax.rem(me // stride, radix))
        stride *= radix

    def peer(level, step):
        radix = radices[level]
        other = lax.rem(digits[level] + step, radix)
        return me + (other - digits[level]) * strides[level], other

    following = lax.rem(me + 1, n_seq)
    before = lax.rem(me + n_seq - 1, n_seq)

    barrier = pltpu.get_barrier_semaphore()
    greeted = 0
    for level in range(levels):
        for step in range(1, radices[level]):
            pl.semaphore_signal(barrier, inc=1, device_id={"seq": peer(level, step)[0]}, device_id_type=MESH)
            greeted += 1
    for other in (following, before):
        pl.semaphore_signal(barrier, inc=1, device_id={"seq": other}, device_id_type=MESH)
        greeted += 1
    for step in range(1, n_head):
        pl.semaphore_signal(
            barrier, inc=1, device_id={"head": lax.rem(head + step, n_head)}, device_id_type=MESH
        )
        greeted += 1

    def prepare(c):
        rate_row = jnp.broadcast_to(rate_ref[c : c + 1, :], (LANES, rows))
        rate = rate_row.T
        rate = jnp.concatenate([rate] * (dh // LANES), axis=1)
        aim = (-(rate * v_ref[c].astype(F32))).astype(BF16)
        target[c] = aim
        for copy in pair_copies(c, 1):
            copy.start()
        target_t[c, :, :rows] = aim.T
        keys_t[c, :, :rows] = k_ref[c].T

    def pair_copies(c, kind):
        made = []
        for step in range(1, ways):
            source, dest = ((k_hbm, k_far), (target, target_far))[kind]
            made.append(
                pltpu.make_async_remote_copy(
                    src_ref=source.at[c], dst_ref=dest.at[c, step - 1],
                    send_sem=pair_send.at[c, kind, step], recv_sem=pair_recv.at[c, kind, step],
                    device_id={"seq": peer(0, step)[0]}, device_id_type=MESH,
                )
            )
        return made

    def prepare_far(c):
        for kind in range(2):
            for copy in pair_copies(c, kind):
                copy.wait()
        for step in range(1, ways):
            place = slice(step * rows, (step + 1) * rows)
            target_t[c, :, place] = target_far[c, step - 1].T
            keys_t[c, :, place] = k_far[c, step - 1].T

    def gradient(c):
        weights = start_b if c == 0 else cur.at[c - 1, 0]
        piece = min(256, rows)
        for slot in range(ways):
            if c == 0 and slot == 1:
                prepare_far(c)
            for start in range(0, rows, piece):
                part = slice(start, start + piece)
                place = slice(slot * rows + start, slot * rows + start + piece)
                k_part = k_ref[c, part] if slot == 0 else k_far[c, slot - 1, part]
                aim = target[c, part] if slot == 0 else target_far[c, slot - 1, part]
                gate_f[place, :] = dot(k_part, weights[0])
                up_f[place, :] = dot(k_part, weights[2])
                back_f[place, :] = dot(aim, weights[1])
                for r in range(place.start, place.start + piece, CHUNK):
                    at = slice(r, r + CHUNK)
                    pre_gate, pre_up, back = gate_f[at, :], up_f[at, :], back_f[at, :]
                    sig = sigmoid(pre_gate)
                    silu = pre_gate * sig
                    hid_s[at, :] = (silu * pre_up).astype(BF16)
                    da_s[at, :] = (back * pre_up * (sig * (1.0 + pre_gate * (1.0 - sig)))).astype(BF16)
                    db_s[at, :] = (back * silu).astype(BF16)
        sent = 0
        for p, (left, right) in enumerate(((target_t, hid_s), (keys_t, da_s), (keys_t, db_s))):
            grad = dot(left[c], right[...])
            for cb in range(cols):
                base = p * matrix_rows + cb * dh
                block = grad[:, cb * LANES : (cb + 1) * LANES]
                acc[base : base + dh, :] = block
                send_b[c, base : base + dh, :] = block.astype(BF16)
            while (sent + 1) * part_rows <= (p + 1) * matrix_rows:
                start_stage(c, sent, 0)
                sent += 1

    def span_of(start, size):
        return pl.ds(pl.multiple_of(start, 16), size)

    def fill(work):
        if work:
            work.pop(0)()

    def owned(unit, level, first):
        start = 0
        for l in range(first, level + 1):
            start = start + digits[l] * (unit * math.prod(radices[l + 1 :]))
        return start

    def gather_copies(buf, offset, unit, level, first, sends, recvs):
        size = unit * math.prod(radices[level + 1 :])
        made = []
        for step in range(1, radices[level]):
            slot = sum(radices[:level]) + step
            block = buf.at[span_of(offset + owned(unit, level, first), size)]
            made.append(
                pltpu.make_async_remote_copy(
                    src_ref=block, dst_ref=block, send_sem=sends.at[slot], recv_sem=recvs.at[slot],
                    device_id={"seq": peer(level, step)[0]}, device_id_type=MESH,
                )
            )
        return made

    unit = part_rows // (n_seq // ways)

    def landing_at(p, level):
        sizes = [unit * math.prod(radices[l + 1 :]) * (radices[l] - 1) for l in range(1, levels)]
        return p * sum(sizes) + sum(sizes[: level - 1])

    def scatter_copies(c, p, level):
        size = unit * math.prod(radices[level + 1 :])
        base = p * part_rows + owned(unit, level - 1, 1)
        made = []
        for step in range(1, radices[level]):
            target_dev, other = peer(level, step)
            slot = sum(radices[:level]) + step
            made.append(
                pltpu.make_async_remote_copy(
                    src_ref=send_b.at[c, span_of(base + other * size, size)],
                    dst_ref=recv_b.at[c, pl.ds(landing_at(p, level) + (step - 1) * size, size)],
                    send_sem=ar_send.at[c, p, slot], recv_sem=ar_recv.at[c, p, slot],
                    device_id={"seq": target_dev}, device_id_type=MESH,
                )
            )
        return made

    halfway = levels - 1
    stages = 2 * halfway

    def stage_copies(c, p, stage):
        if stage < halfway:
            return scatter_copies(c, p, stage + 1)
        return gather_copies(
            full_b.at[c], p * part_rows, unit, stages - stage, 1, ag_send.at[c, p], ag_recv.at[c, p]
        )

    def start_stage(c, p, stage):
        for copy in stage_copies(c, p, stage):
            copy.start()

    def squares_of(value):
        return jnp.sum((value * value).reshape(value.shape[0] // 8, 8, LANES), axis=0)

    def finish_stage(c, p, stage):
        for copy in stage_copies(c, p, stage):
            copy.wait_recv()
        if stage < halfway:
            level = stage + 1
            size = unit * math.prod(radices[level + 1 :])
            place = span_of(p * part_rows + owned(unit, level, 1), size)
            mine = acc[place, :]
            landed = landing_at(p, level)
            for step in range(radices[level] - 1):
                mine += recv_b[c, landed + step * size : landed + (step + 1) * size, :].astype(F32)
            if level < levels - 1:
                acc[place, :] = mine
                send_b[c, place, :] = mine.astype(BF16)
            else:
                full_b[c, place, :] = mine.astype(BF16)
        if stage + 1 < stages:
            start_stage(c, p, stage + 1)

    def norm_copies(c):
        made = []
        for step in range(1, ways):
            made.append(
                pltpu.make_async_remote_copy(
                    src_ref=sq_out.at[c], dst_ref=sq_in.at[c, step],
                    send_sem=sq_send.at[c, step], recv_sem=sq_recv.at[c, step],
                    device_id={"seq": peer(0, step)[0]}, device_id_type=MESH,
                )
            )
        return made

    def all_reduce(c, work):
        squares = jnp.zeros((8, LANES), F32)
        for key in range(stages + parts - 1):
            fill(work)
            for p in reversed(range(parts)):
                stage = key - p
                if 0 <= stage < stages:
                    finish_stage(c, p, stage)
                    if stage == stages - 1:
                        for r in range(p * part_rows, (p + 1) * part_rows, 128):
                            squares += squares_of(full_b[c, r : r + 128, :].astype(F32))
        sq_out[c] = squares
        for copy in norm_copies(c):
            copy.start()
        while work:
            fill(work)
        for step, copy in enumerate(norm_copies(c)):
            copy.wait()
            squares = squares + sq_in[c, step + 1]
        return squares

    def settle(c):
        for p in range(parts):
            for stage in range(stages):
                for copy in stage_copies(c, p, stage):
                    copy.wait_send()

    def cur_copies(c):
        made = []
        for step in range(1, ways):
            made.append(
                pltpu.make_async_remote_copy(
                    src_ref=cur.at[c, 0], dst_ref=cur.at[c, step],
                    send_sem=cur_send.at[c, step], recv_sem=cur_recv.at[c, step],
                    device_id={"seq": peer(0, step)[0]}, device_id_type=MESH,
                )
            )
        return made

    def update(c, squares):
        whole = jnp.sum(jnp.sum(squares, axis=1, keepdims=True), axis=0, keepdims=True)
        factor = jnp.minimum(1.0, 0.6 * math.sqrt(hid) / jnp.sqrt(whole + 1e-6))
        for p, m in ((1, 0), (2, 2), (0, 1)):
            for cb in range(cols):
                base = p * matrix_rows + cb * dh
                lanes = slice(cb * LANES, (cb + 1) * LANES)
                for r in range(0, dh, 64):
                    at = slice(r, r + 64)
                    change = factor * full_b[c, base + r : base + r + 64, :].astype(F32)
                    if c > 0:
                        change = MOMENTUM * mom[m, at, lanes] + change
                    fresh = wts[m][at, lanes] - change
                    if c < spans - 1:
                        mom[m, at, lanes] = change
                        wts[m][at, lanes] = fresh
                    cur[c, 0, m, at, lanes] = fresh.astype(BF16)
        for copy in cur_copies(c):
            copy.start()

    scale = 1.0 / math.sqrt(dh)

    def attend(c, j):
        start = j * WINDOW
        here = slice(start, start + WINDOW)
        if j == 0:
            first = me == 0
            span = jnp.where(first, (c + spans - 1) % spans, c)
            left_k, left_v = edge_k[span], edge_v[span]
        else:
            earlier = slice(start - WINDOW, start)
            left_k, left_v = k_ref[c, earlier], v_ref[c, earlier]
        query = q_ref[c, here]
        score_f[:, :WINDOW] = dot_t(query, left_k)
        score_f[:, WINDOW:] = dot_t(query, k_ref[c, here])
        for r in range(0, WINDOW, CHUNK):
            at = slice(r, r + CHUNK)
            row_ids = lax.broadcasted_iota(jnp.int32, (CHUNK, 2 * WINDOW), 0) + r
            col_ids = lax.broadcasted_iota(jnp.int32, (CHUNK, 2 * WINDOW), 1)
            lowest = row_ids
            if j == 0 and c == 0:
                lowest = jnp.maximum(lowest, jnp.where(me == 0, WINDOW - 1, 0))
            ok = (col_ids > lowest) & (col_ids <= row_ids + WINDOW)
            scores = jnp.where(ok, score_f[at, :] * scale, -1e30)
            scores = jnp.exp(scores - jnp.max(scores, axis=1, keepdims=True))
            share = 1.0 / jnp.sum(scores, axis=1, keepdims=True)
            prob_s[at, :] = (scores * share).astype(BF16)
        win[c, here] = dot(prob_s[:, :WINDOW], left_v) + dot(prob_s[:, WINDOW:], v_ref[c, here])

    half = WINDOW

    def mix_copies(c, j):
        made = []
        for step in range(1, n_head):
            block = mix.at[head, c, pl.ds(j * half, half)]
            made.append(
                pltpu.make_async_remote_copy(
                    src_ref=block, dst_ref=block,
                    send_sem=mix_send.at[c, j, step], recv_sem=mix_recv.at[c, j, step],
                    device_id={"head": lax.rem(head + step, n_head)}, device_id_type=MESH,
                )
            )
        return made

    def fast_part(c, j, slot):
        query = q_ref[c, j * half : (j + 1) * half]
        gate_f[:half, :] = dot(query, cur[c, slot, 0])
        up_f[:half, :] = dot(query, cur[c, slot, 2])
        for r in range(0, half, CHUNK):
            at = slice(r, r + CHUNK)
            pre_gate = gate_f[at, :]
            hidden_s[at, :] = (pre_gate * sigmoid(pre_gate) * up_f[at, :]).astype(BF16)
        return dot_t(hidden_s[...], cur[c, slot, 1])

    def apply_near(c, j):
        near[c, j * half : (j + 1) * half] = fast_part(c, j, 0)

    def apply_far(c, j):
        part = slice(j * half, (j + 1) * half)
        if j == 0:
            for copy in cur_copies(c):
                copy.wait()
        for slot in range(1, ways):
            near[c, part] += fast_part(c, j, slot)
        for r in range(0, half, CHUNK):
            at = slice(j * half + r, j * half + r + CHUNK)
            fast = near[c, at]
            norm = fast * lax.rsqrt(jnp.mean(fast * fast, axis=-1, keepdims=True) + 1e-5)
            mix[head, c, at] = (norm + win[c, at]).astype(BF16)
        for copy in mix_copies(c, j):
            copy.start()

    def apply(c, j):
        apply_near(c, j)
        apply_far(c, j)

    def project(c, j):
        part = slice(j * half, (j + 1) * half)
        for copy in mix_copies(c, j):
            copy.wait()
        result = None
        for h in range(n_head):
            term = dot_t(mix[h, c, part], ow_t[:, h * dh : (h + 1) * dh])
            result = term if result is None else result + term
        out_ref[c, part] = result.astype(BF16)

    halo = []
    for index, (source, dest) in enumerate(((k_hbm, edge_k), (v_hbm, edge_v))):
        for c in range(spans):
            halo.append(
                pltpu.make_async_remote_copy(
                    src_ref=source.at[c, pl.ds(rows - WINDOW, WINDOW)], dst_ref=dest.at[c],
                    send_sem=halo_send.at[index, c], recv_sem=halo_recv.at[index, c],
                    device_id={"seq": following}, device_id_type=MESH,
                )
            )

    shard = ow_ref.shape[0]

    def weight_copies(level):
        return gather_copies(ow_all, 0, shard, level, 0, ow_send, ow_recv)

    def weight_next(level):
        if level < levels - 1:
            for copy in weight_copies(level + 1):
                copy.wait()
        for copy in weight_copies(level):
            copy.start()

    def weight_end():
        for copy in weight_copies(0):
            copy.wait()
        for s in range(n_seq):
            place, rest = 0, s
            for radix in radices:
                place = place * radix + rest % radix
                rest //= radix
            ow_t[s * shard : (s + 1) * shard, :] = ow_all[place * shard : (place + 1) * shard, :]

    tiles = rows // WINDOW
    pl.semaphore_wait(barrier, greeted)
    for c in range(spans):
        for copy in pair_copies(c, 0):
            copy.start()
        if c == 0:
            for copy in halo:
                copy.start()
    loads["rate"].wait()
    loads[("k", 0)].wait()
    loads[("v", 0)].wait()
    prepare(0)
    loads["gate"].wait()
    start_b[0] = gate_w[...].astype(BF16)
    loads["up"].wait()
    start_b[2] = up_w[...].astype(BF16)
    loads["down"].wait()
    down_w[...] = down_ref[...].T
    start_b[1] = down_w[...].astype(BF16)
    loads["ow"].wait()
    if gather_weight:
        ow_all[span_of(owned(shard, levels - 1, 0), shard), :] = ow_ref[...]
        weight_next(levels - 1)
    else:
        ow_t[...] = ow_ref[...]
    gradient(0)
    loads["q"].wait()
    for c in range(1, spans):
        loads[("k", c)].wait()
        loads[("v", c)].wait()
    for c in range(spans):
        work = []
        if c + 1 < spans:
            work.append(functools.partial(prepare, c + 1))
        if c == 0:
            work += [functools.partial(attend, s, j) for s in range(spans) for j in range(1, tiles)]

            def edges():
                for copy in halo:
                    copy.wait()
                attend(0, 0)

            work.append(edges)
            work += [functools.partial(attend, s, 0) for s in range(1, spans)]
        if c + 1 < spans:
            work.append(functools.partial(prepare_far, c + 1))
        if c > 0:
            work += [functools.partial(apply, c - 1, j) for j in range(tiles)]
        if c == spans - 1:
            if gather_weight:
                first = levels - 2 if c > 0 else levels - 1
                work += [functools.partial(weight_next, level) for level in reversed(range(first))]
                work.append(weight_end)
            work += [functools.partial(project, s, j) for s in range(c) for j in range(tiles)]
        update(c, all_reduce(c, work))
        if c + 1 < spans:
            if c + 1 == spans - 1 and gather_weight and levels > 1:
                weight_next(levels - 2)
            gradient(c + 1)
    for j in range(tiles):
        apply_near(spans - 1, j)
    for j in range(tiles):
        apply_far(spans - 1, j)
    for j in range(tiles):
        project(spans - 1, j)
    for c in range(spans):
        settle(c)


def body(n_seq, n_head, queries, key_rows, values, learn_rates, fast_gate, fast_down, fast_up, output_weight):
    spans, rows, _, dh = queries.shape
    hid = fast_gate.shape[2]
    features, shard = output_weight.shape
    gather_weight = shard % 16 == 0
    if gather_weight:
        weight = output_weight.T
    else:
        weight = lax.all_gather(output_weight, "seq", axis=1, tiled=True).T
    out_cols = shard * n_seq
    radices = radices_of(n_seq)
    ways = radices[0]
    hid_part = hid // ways
    cols = hid_part // LANES
    total = 3 * cols * dh
    landing, size = 0, total
    for radix in radices[1:]:
        size //= radix
        landing += (radix - 1) * size
    parts = parts_of(total, n_seq // ways)
    slots = sum(radices) + 1
    tiles = rows // WINDOW
    dma = pltpu.SemaphoreType.DMA
    vmem = pltpu.VMEM
    return pl.pallas_call(
        functools.partial(kernel, n_seq, n_head, gather_weight),
        out_shape=jax.ShapeDtypeStruct((spans, rows, out_cols), BF16),
        in_specs=[pl.BlockSpec(memory_space=pltpu.HBM)] * 8,
        out_specs=pl.BlockSpec(memory_space=pltpu.VMEM),
        scratch_shapes=[
            vmem((spans, rows, dh), BF16),
            vmem((spans, rows, dh), BF16),
            vmem((spans, rows, dh), BF16),
            vmem((spans, rows), F32),
            vmem((dh, hid_part), F32),
            vmem((hid_part, dh), F32),
            vmem((dh, hid_part), F32),
            vmem(weight.shape, BF16),
            vmem((dh, hid_part), F32),
            vmem((3, dh, hid_part), F32),
            vmem((3, dh, hid_part), BF16),
            vmem((spans, ways, 3, dh, hid_part), BF16),
            vmem((spans, dh, ways * rows), BF16),
            vmem((spans, rows, dh), BF16),
            vmem((spans, dh, ways * rows), BF16),
            vmem((spans, ways - 1, rows, dh), BF16),
            vmem((spans, ways - 1, rows, dh), BF16),
            vmem((ways * rows, hid_part), BF16),
            vmem((ways * rows, hid_part), BF16),
            vmem((ways * rows, hid_part), BF16),
            vmem((ways * rows, hid_part), F32),
            vmem((ways * rows, hid_part), F32),
            vmem((ways * rows, hid_part), F32),
            vmem((WINDOW, 2 * WINDOW), F32),
            vmem((WINDOW, 2 * WINDOW), BF16),
            vmem((WINDOW, hid_part), BF16),
            vmem((WINDOW, dh), F32),
            vmem((total, LANES), F32),
            vmem((spans, total, LANES), BF16),
            vmem((spans, landing, LANES), BF16),
            vmem((spans, total, LANES), BF16),
            vmem((spans, 8, LANES), F32),
            vmem((spans, ways, 8, LANES), F32),
            vmem((spans, WINDOW, dh), BF16),
            vmem((spans, WINDOW, dh), BF16),
            vmem((out_cols, features), BF16),
            vmem((out_cols, features), BF16),
            vmem((n_head, spans, rows, dh), BF16),
            vmem((spans, rows, dh), F32),
            vmem((spans, rows, dh), F32),
            dma((6 + 2 * spans,)),
            dma((spans, 2, ways)),
            dma((spans, 2, ways)),
            dma((spans, ways)),
            dma((spans, ways)),
            dma((spans, ways)),
            dma((spans, ways)),
            dma((spans, parts, slots)),
            dma((spans, parts, slots)),
            dma((spans, parts, slots)),
            dma((spans, parts, slots)),
            dma((2, spans)),
            dma((2, spans)),
            dma((slots,)),
            dma((slots,)),
            dma((spans, tiles, n_head)),
            dma((spans, tiles, n_head)),
        ],
        compiler_params=pltpu.CompilerParams(
            collective_id=0, has_side_effects=True, vmem_limit_bytes=60 * 1024 * 1024
        ),
    )(
        queries[:, :, 0, :], key_rows[:, :, 0, :], values[:, :, 0, :], learn_rates[0],
        fast_gate[0], fast_down[0], fast_up[0], weight,
    )


def solution(mesh):
    placed = (
        P(None, "seq", "head", None),
        P(None, "seq", "head", None),
        P(None, "seq", "head", None),
        P("head", None, "seq"),
        P("head", None, None),
        P("head", None, None),
        P("head", None, None),
        P(None, ("head", "seq")),
    )
    return jax.shard_map(
        functools.partial(body, mesh.shape["seq"], mesh.shape["head"]),
        mesh=mesh, in_specs=placed, out_specs=P(None, "seq", "head"), check_vma=False,
    )
```

```python
import functools
import math

import jax
import jax.numpy as jnp
from jax import lax
from jax.experimental import pallas as pl
from jax.experimental.pallas import tpu as pltpu
from jax.sharding import PartitionSpec as P

WINDOW = 256
MOMENTUM = 0.9
LANES = 128
CHUNK = 16
PARTS = 1
MESH = pl.DeviceIdType.MESH
F32 = jnp.float32
BF16 = jnp.bfloat16


def radices_of(count):
    found = []
    while count > 1:
        if count % 2:
            found.append(count)
        elif len(found) < 2 or count % 4:
            found.append(2)
        else:
            found.append(4)
        count //= found[-1]
    return found


def parts_of(rows, holders):
    return PARTS if rows % (PARTS * holders * 16) == 0 else 1


def dot(left, right):
    return jnp.dot(left, right, preferred_element_type=F32)


def dot_t(left, right):
    return lax.dot_general(left, right, (((1,), (1,)), ((), ())), preferred_element_type=F32)


def sigmoid(value):
    return 0.5 * jnp.tanh(0.5 * value) + 0.5


def kernel(
    n_seq, n_head, gather_weight,
    q_hbm, k_hbm, v_hbm, rate_hbm, gate_hbm, down_hbm, up_hbm, ow_hbm,
    out_ref,
    q_ref, k_ref, v_ref, rate_ref, gate_w, down_ref, up_w, ow_ref, down_w,
    mom, start_b, cur, keys_t, target, target_t, k_far, target_far, hid_s, da_s, db_s,
    gate_f, up_f, back_f, score_f, prob_s, hidden_s, fast_f,
    acc, send_b, recv_b, full_b, sq_out, sq_in, edge_k, edge_v, ow_all, ow_t, mix, win, near,
    load_sem, pair_send, pair_recv, cur_send, cur_recv, sq_send, sq_recv, ar_send, ar_recv, ag_send, ag_recv, halo_send, halo_recv, ow_send, ow_recv, mix_send, mix_recv,
):
    spans, rows, dh = q_ref.shape
    hid = gate_hbm.shape[1]
    ways = radices_of(n_seq)[0]
    hid_part = hid // ways
    cols = hid_part // LANES
    matrix_rows = cols * dh
    parts = parts_of(3 * matrix_rows, n_seq // ways)
    part_rows = 3 * matrix_rows // parts
    wts = (gate_w, down_w, up_w)
    radices = radices_of(n_seq)
    levels = len(radices)
    me = lax.axis_index("seq")
    head = lax.axis_index("head")
    share = pl.ds(pl.multiple_of(lax.rem(me, ways) * hid_part, hid_part), hid_part)

    loads = {}

    def load(name, source, dest):
        loads[name] = pltpu.make_async_copy(source, dest, load_sem.at[len(loads)])
        loads[name].start()

    load("gate", gate_hbm.at[:, share], gate_w)
    load(("k", 0), k_hbm.at[0], k_ref.at[0])
    load("up", up_hbm.at[:, share], up_w)
    load("rate", rate_hbm, rate_ref)
    load(("v", 0), v_hbm.at[0], v_ref.at[0])
    load("down", down_hbm.at[share], down_ref)
    load("ow", ow_hbm, ow_ref)
    for c in range(1, spans):
        load(("k", c), k_hbm.at[c], k_ref.at[c])
        load(("v", c), v_hbm.at[c], v_ref.at[c])
    load("q", q_hbm, q_ref)

    strides, digits = [], []
    stride = 1
    for radix in radices:
        strides.append(stride)
        digits.append(lax.rem(me // stride, radix))
        stride *= radix

    def peer(level, step):
        radix = radices[level]
        other = lax.rem(digits[level] + step, radix)
        return me + (other - digits[level]) * strides[level], other

    following = lax.rem(me + 1, n_seq)
    before = lax.rem(me + n_seq - 1, n_seq)

    barrier = pltpu.get_barrier_semaphore()
    greeted = 0
    for level in range(levels):
        for step in range(1, radices[level]):
            pl.semaphore_signal(barrier, inc=1, device_id={"seq": peer(level, step)[0]}, device_id_type=MESH)
            greeted += 1
    for other in (following, before):
        pl.semaphore_signal(barrier, inc=1, device_id={"seq": other}, device_id_type=MESH)
        greeted += 1
    for step in range(1, n_head):
        pl.semaphore_signal(
            barrier, inc=1, device_id={"head": lax.rem(head + step, n_head)}, device_id_type=MESH
        )
        greeted += 1

    def prepare(c):
        rate_row = jnp.broadcast_to(rate_ref[c : c + 1, :], (LANES, rows))
        rate = rate_row.T
        rate = jnp.concatenate([rate] * (dh // LANES), axis=1)
        aim = (-(rate * v_ref[c].astype(F32))).astype(BF16)
        target[c] = aim
        for copy in pair_copies(c, 1):
            copy.start()
        target_t[c, :, :rows] = aim.T
        keys_t[c, :, :rows] = k_ref[c].T

    def pair_copies(c, kind):
        made = []
        for step in range(1, ways):
            source, dest = ((k_hbm, k_far), (target, target_far))[kind]
            made.append(
                pltpu.make_async_remote_copy(
                    src_ref=source.at[c], dst_ref=dest.at[c, step - 1],
                    send_sem=pair_send.at[c, kind, step], recv_sem=pair_recv.at[c, kind, step],
                    device_id={"seq": peer(0, step)[0]}, device_id_type=MESH,
                )
            )
        return made

    def prepare_far(c):
        for kind in range(2):
            for copy in pair_copies(c, kind):
                copy.wait()
        for step in range(1, ways):
            place = slice(step * rows, (step + 1) * rows)
            target_t[c, :, place] = target_far[c, step - 1].T
            keys_t[c, :, place] = k_far[c, step - 1].T

    def gradient(c):
        weights = start_b if c == 0 else cur.at[c - 1, 0]
        piece = min(256, rows)
        for slot in range(ways):
            if c == 0 and slot == 1:
                prepare_far(c)
            for start in range(0, rows, piece):
                part = slice(start, start + piece)
                place = slice(slot * rows + start, slot * rows + start + piece)
                k_part = k_ref[c, part] if slot == 0 else k_far[c, slot - 1, part]
                aim = target[c, part] if slot == 0 else target_far[c, slot - 1, part]
                gate_f[place, :] = dot(k_part, weights[0])
                up_f[place, :] = dot(k_part, weights[2])
                back_f[place, :] = dot(aim, weights[1])
                for r in range(place.start, place.start + piece, CHUNK):
                    at = slice(r, r + CHUNK)
                    pre_gate, pre_up, back = gate_f[at, :], up_f[at, :], back_f[at, :]
                    sig = sigmoid(pre_gate)
                    silu = pre_gate * sig
                    hid_s[at, :] = (silu * pre_up).astype(BF16)
                    da_s[at, :] = (back * pre_up * (sig * (1.0 + pre_gate * (1.0 - sig)))).astype(BF16)
                    db_s[at, :] = (back * silu).astype(BF16)
        sent = 0
        for p, (left, right) in enumerate(((target_t, hid_s), (keys_t, da_s), (keys_t, db_s))):
            grad = dot(left[c], right[...])
            for cb in range(cols):
                base = p * matrix_rows + cb * dh
                block = grad[:, cb * LANES : (cb + 1) * LANES]
                acc[base : base + dh, :] = block
                send_b[c, base : base + dh, :] = block.astype(BF16)
            while (sent + 1) * part_rows <= (p + 1) * matrix_rows:
                start_stage(c, sent, 0)
                sent += 1

    def span_of(start, size):
        return pl.ds(pl.multiple_of(start, 16), size)

    def fill(work):
        if work:
            work.pop(0)()

    def owned(unit, level, first):
        start = 0
        for l in range(first, level + 1):
            start = start + digits[l] * (unit * math.prod(radices[l + 1 :]))
        return start

    def gather_copies(buf, offset, unit, level, first, sends, recvs):
        size = unit * math.prod(radices[level + 1 :])
        made = []
        for step in range(1, radices[level]):
            slot = sum(radices[:level]) + step
            block = buf.at[span_of(offset + owned(unit, level, first), size)]
            made.append(
                pltpu.make_async_remote_copy(
                    src_ref=block, dst_ref=block, send_sem=sends.at[slot], recv_sem=recvs.at[slot],
                    device_id={"seq": peer(level, step)[0]}, device_id_type=MESH,
                )
            )
        return made

    unit = part_rows // (n_seq // ways)

    def landing_at(p, level):
        sizes = [unit * math.prod(radices[l + 1 :]) * (radices[l] - 1) for l in range(1, levels)]
        return p * sum(sizes) + sum(sizes[: level - 1])

    def scatter_copies(c, p, level):
        size = unit * math.prod(radices[level + 1 :])
        base = p * part_rows + owned(unit, level - 1, 1)
        made = []
        for step in range(1, radices[level]):
            target_dev, other = peer(level, step)
            slot = sum(radices[:level]) + step
            made.append(
                pltpu.make_async_remote_copy(
                    src_ref=send_b.at[c, span_of(base + other * size, size)],
                    dst_ref=recv_b.at[c, pl.ds(landing_at(p, level) + (step - 1) * size, size)],
                    send_sem=ar_send.at[c, p, slot], recv_sem=ar_recv.at[c, p, slot],
                    device_id={"seq": target_dev}, device_id_type=MESH,
                )
            )
        return made

    halfway = levels - 1
    stages = 2 * halfway

    def stage_copies(c, p, stage):
        if stage < halfway:
            return scatter_copies(c, p, stage + 1)
        return gather_copies(
            full_b.at[c], p * part_rows, unit, stages - stage, 1, ag_send.at[c, p], ag_recv.at[c, p]
        )

    def start_stage(c, p, stage):
        for copy in stage_copies(c, p, stage):
            copy.start()

    def squares_of(value):
        return jnp.sum((value * value).reshape(value.shape[0] // 8, 8, LANES), axis=0)

    def finish_stage(c, p, stage):
        for copy in stage_copies(c, p, stage):
            copy.wait_recv()
        if stage < halfway:
            level = stage + 1
            size = unit * math.prod(radices[level + 1 :])
            place = span_of(p * part_rows + owned(unit, level, 1), size)
            mine = acc[place, :]
            landed = landing_at(p, level)
            for step in range(radices[level] - 1):
                mine += recv_b[c, landed + step * size : landed + (step + 1) * size, :].astype(F32)
            if level < levels - 1:
                acc[place, :] = mine
                send_b[c, place, :] = mine.astype(BF16)
            else:
                full_b[c, place, :] = mine.astype(BF16)
        if stage + 1 < stages:
            start_stage(c, p, stage + 1)

    def norm_copies(c):
        made = []
        for step in range(1, ways):
            made.append(
                pltpu.make_async_remote_copy(
                    src_ref=sq_out.at[c], dst_ref=sq_in.at[c, step],
                    send_sem=sq_send.at[c, step], recv_sem=sq_recv.at[c, step],
                    device_id={"seq": peer(0, step)[0]}, device_id_type=MESH,
                )
            )
        return made

    def all_reduce(c, work):
        squares = jnp.zeros((8, LANES), F32)
        groups = stages + parts - 1
        for key in range(groups):
            for _ in range(-(-len(work) // (groups - key))):
                fill(work)
            for p in reversed(range(parts)):
                stage = key - p
                if 0 <= stage < stages:
                    finish_stage(c, p, stage)
                    if stage == stages - 1:
                        for r in range(p * part_rows, (p + 1) * part_rows, 128):
                            squares += squares_of(full_b[c, r : r + 128, :].astype(F32))
        sq_out[c] = squares
        for copy in norm_copies(c):
            copy.start()
        while work:
            fill(work)
        for step, copy in enumerate(norm_copies(c)):
            copy.wait()
            squares = squares + sq_in[c, step + 1]
        return squares

    def settle(c):
        for p in range(parts):
            for stage in range(stages):
                for copy in stage_copies(c, p, stage):
                    copy.wait_send()

    def cur_copies(c):
        made = []
        for step in range(1, ways):
            made.append(
                pltpu.make_async_remote_copy(
                    src_ref=cur.at[c, 0], dst_ref=cur.at[c, step],
                    send_sem=cur_send.at[c, step], recv_sem=cur_recv.at[c, step],
                    device_id={"seq": peer(0, step)[0]}, device_id_type=MESH,
                )
            )
        return made

    def update(c, squares):
        whole = jnp.sum(jnp.sum(squares, axis=1, keepdims=True), axis=0, keepdims=True)
        factor = jnp.minimum(1.0, 0.6 * math.sqrt(hid) / jnp.sqrt(whole + 1e-6))
        for p, m in ((1, 0), (2, 2), (0, 1)):
            for cb in range(cols):
                base = p * matrix_rows + cb * dh
                lanes = slice(cb * LANES, (cb + 1) * LANES)
                for r in range(0, dh, 64):
                    at = slice(r, r + 64)
                    change = factor * full_b[c, base + r : base + r + 64, :].astype(F32)
                    if c > 0:
                        change = MOMENTUM * mom[m, at, lanes] + change
                    fresh = wts[m][at, lanes] - change
                    if c < spans - 1:
                        mom[m, at, lanes] = change
                        wts[m][at, lanes] = fresh
                    cur[c, 0, m, at, lanes] = fresh.astype(BF16)
        for copy in cur_copies(c):
            copy.start()

    scale = 1.0 / math.sqrt(dh)

    def attend(c, j):
        start = j * WINDOW
        here = slice(start, start + WINDOW)
        if j == 0:
            first = me == 0
            span = jnp.where(first, (c + spans - 1) % spans, c)
            left_k, left_v = edge_k[span], edge_v[span]
        else:
            earlier = slice(start - WINDOW, start)
            left_k, left_v = k_ref[c, earlier], v_ref[c, earlier]
        query = q_ref[c, here]
        score_f[:, :WINDOW] = dot_t(query, left_k)
        score_f[:, WINDOW:] = dot_t(query, k_ref[c, here])
        for r in range(0, WINDOW, CHUNK):
            at = slice(r, r + CHUNK)
            row_ids = lax.broadcasted_iota(jnp.int32, (CHUNK, 2 * WINDOW), 0) + r
            col_ids = lax.broadcasted_iota(jnp.int32, (CHUNK, 2 * WINDOW), 1)
            lowest = row_ids
            if j == 0 and c == 0:
                lowest = jnp.maximum(lowest, jnp.where(me == 0, WINDOW - 1, 0))
            ok = (col_ids > lowest) & (col_ids <= row_ids + WINDOW)
            scores = jnp.where(ok, score_f[at, :] * scale, -1e30)
            scores = jnp.exp(scores - jnp.max(scores, axis=1, keepdims=True))
            share = 1.0 / jnp.sum(scores, axis=1, keepdims=True)
            prob_s[at, :] = (scores * share).astype(BF16)
        win[c, here] = dot(prob_s[:, :WINDOW], left_v) + dot(prob_s[:, WINDOW:], v_ref[c, here])

    half = WINDOW

    def mix_copies(c, j):
        made = []
        for step in range(1, n_head):
            block = mix.at[head, c, pl.ds(j * half, half)]
            made.append(
                pltpu.make_async_remote_copy(
                    src_ref=block, dst_ref=block,
                    send_sem=mix_send.at[c, j, step], recv_sem=mix_recv.at[c, j, step],
                    device_id={"head": lax.rem(head + step, n_head)}, device_id_type=MESH,
                )
            )
        return made

    def fast_part(c, j, slot):
        query = q_ref[c, j * half : (j + 1) * half]
        gate_f[:half, :] = dot(query, cur[c, slot, 0])
        up_f[:half, :] = dot(query, cur[c, slot, 2])
        for r in range(0, half, CHUNK):
            at = slice(r, r + CHUNK)
            pre_gate = gate_f[at, :]
            hidden_s[at, :] = (pre_gate * sigmoid(pre_gate) * up_f[at, :]).astype(BF16)
        return dot_t(hidden_s[...], cur[c, slot, 1])

    def apply_near(c, j):
        near[c, j * half : (j + 1) * half] = fast_part(c, j, 0)

    def apply_far(c, j):
        part = slice(j * half, (j + 1) * half)
        if j == 0:
            for copy in cur_copies(c):
                copy.wait()
        for slot in range(1, ways):
            near[c, part] += fast_part(c, j, slot)
        for r in range(0, half, CHUNK):
            at = slice(j * half + r, j * half + r + CHUNK)
            fast = near[c, at]
            norm = fast * lax.rsqrt(jnp.mean(fast * fast, axis=-1, keepdims=True) + 1e-5)
            mix[head, c, at] = (norm + win[c, at]).astype(BF16)
        for copy in mix_copies(c, j):
            copy.start()

    def apply(c, j):
        apply_near(c, j)
        apply_far(c, j)

    def project(c, j):
        part = slice(j * half, (j + 1) * half)
        for copy in mix_copies(c, j):
            copy.wait()
        result = None
        for h in range(n_head):
            term = dot_t(mix[h, c, part], ow_t[:, h * dh : (h + 1) * dh])
            result = term if result is None else result + term
        out_ref[c, part] = result.astype(BF16)

    halo = []
    for index, (source, dest) in enumerate(((k_hbm, edge_k), (v_hbm, edge_v))):
        for c in range(spans):
            halo.append(
                pltpu.make_async_remote_copy(
                    src_ref=source.at[c, pl.ds(rows - WINDOW, WINDOW)], dst_ref=dest.at[c],
                    send_sem=halo_send.at[index, c], recv_sem=halo_recv.at[index, c],
                    device_id={"seq": following}, device_id_type=MESH,
                )
            )

    shard = ow_ref.shape[0]

    def weight_copies(level):
        return gather_copies(ow_all, 0, shard, level, 0, ow_send, ow_recv)

    def weight_next(level):
        if level < levels - 1:
            for copy in weight_copies(level + 1):
                copy.wait()
        for copy in weight_copies(level):
            copy.start()

    def weight_end():
        for copy in weight_copies(0):
            copy.wait()
        for s in range(n_seq):
            place, rest = 0, s
            for radix in radices:
                place = place * radix + rest % radix
                rest //= radix
            ow_t[s * shard : (s + 1) * shard, :] = ow_all[place * shard : (place + 1) * shard, :]

    tiles = rows // WINDOW
    pl.semaphore_wait(barrier, greeted)
    for c in range(spans):
        for copy in pair_copies(c, 0):
            copy.start()
        if c == 0:
            for copy in halo:
                copy.start()
    loads["rate"].wait()
    loads[("k", 0)].wait()
    loads[("v", 0)].wait()
    prepare(0)
    loads["gate"].wait()
    start_b[0] = gate_w[...].astype(BF16)
    loads["up"].wait()
    start_b[2] = up_w[...].astype(BF16)
    loads["down"].wait()
    down_w[...] = down_ref[...].T
    start_b[1] = down_w[...].astype(BF16)
    loads["ow"].wait()
    if gather_weight:
        ow_all[span_of(owned(shard, levels - 1, 0), shard), :] = ow_ref[...]
        weight_next(levels - 1)
    else:
        ow_t[...] = ow_ref[...]
    gradient(0)
    loads["q"].wait()
    for c in range(1, spans):
        loads[("k", c)].wait()
        loads[("v", c)].wait()
    for c in range(spans):
        work = []
        if c + 1 < spans:
            work.append(functools.partial(prepare, c + 1))
        if c == 0:
            work += [functools.partial(attend, s, j) for s in range(spans) for j in range(1, tiles)]

            def edges():
                for copy in halo:
                    copy.wait()
                attend(0, 0)

            work.append(edges)
            work += [functools.partial(attend, s, 0) for s in range(1, spans)]
        if c + 1 < spans:
            work.append(functools.partial(prepare_far, c + 1))
        if c > 0:
            work += [functools.partial(apply, c - 1, j) for j in range(tiles)]
        if c == spans - 1:
            if gather_weight:
                first = levels - 2 if c > 0 else levels - 1
                work += [functools.partial(weight_next, level) for level in reversed(range(first))]
                work.append(weight_end)
            work += [functools.partial(project, s, j) for s in range(c) for j in range(tiles)]
        update(c, all_reduce(c, work))
        if c + 1 < spans:
            if c + 1 == spans - 1 and gather_weight and levels > 1:
                weight_next(levels - 2)
            gradient(c + 1)
    for j in range(tiles):
        apply_near(spans - 1, j)
    for j in range(tiles):
        apply_far(spans - 1, j)
    for j in range(tiles):
        project(spans - 1, j)
    for c in range(spans):
        settle(c)


def body(n_seq, n_head, queries, key_rows, values, learn_rates, fast_gate, fast_down, fast_up, output_weight):
    spans, rows, _, dh = queries.shape
    hid = fast_gate.shape[2]
    features, shard = output_weight.shape
    gather_weight = shard % 16 == 0
    if gather_weight:
        weight = output_weight.T
    else:
        weight = lax.all_gather(output_weight, "seq", axis=1, tiled=True).T
    out_cols = shard * n_seq
    radices = radices_of(n_seq)
    ways = radices[0]
    hid_part = hid // ways
    cols = hid_part // LANES
    total = 3 * cols * dh
    landing, size = 0, total
    for radix in radices[1:]:
        size //= radix
        landing += (radix - 1) * size
    parts = parts_of(total, n_seq // ways)
    slots = sum(radices) + 1
    tiles = rows // WINDOW
    dma = pltpu.SemaphoreType.DMA
    vmem = pltpu.VMEM
    return pl.pallas_call(
        functools.partial(kernel, n_seq, n_head, gather_weight),
        out_shape=jax.ShapeDtypeStruct((spans, rows, out_cols), BF16),
        in_specs=[pl.BlockSpec(memory_space=pltpu.HBM)] * 8,
        out_specs=pl.BlockSpec(memory_space=pltpu.VMEM),
        scratch_shapes=[
            vmem((spans, rows, dh), BF16),
            vmem((spans, rows, dh), BF16),
            vmem((spans, rows, dh), BF16),
            vmem((spans, rows), F32),
            vmem((dh, hid_part), F32),
            vmem((hid_part, dh), F32),
            vmem((dh, hid_part), F32),
            vmem(weight.shape, BF16),
            vmem((dh, hid_part), F32),
            vmem((3, dh, hid_part), F32),
            vmem((3, dh, hid_part), BF16),
            vmem((spans, ways, 3, dh, hid_part), BF16),
            vmem((spans, dh, ways * rows), BF16),
            vmem((spans, rows, dh), BF16),
            vmem((spans, dh, ways * rows), BF16),
            vmem((spans, ways - 1, rows, dh), BF16),
            vmem((spans, ways - 1, rows, dh), BF16),
            vmem((ways * rows, hid_part), BF16),
            vmem((ways * rows, hid_part), BF16),
            vmem((ways * rows, hid_part), BF16),
            vmem((ways * rows, hid_part), F32),
            vmem((ways * rows, hid_part), F32),
            vmem((ways * rows, hid_part), F32),
            vmem((WINDOW, 2 * WINDOW), F32),
            vmem((WINDOW, 2 * WINDOW), BF16),
            vmem((WINDOW, hid_part), BF16),
            vmem((WINDOW, dh), F32),
            vmem((total, LANES), F32),
            vmem((spans, total, LANES), BF16),
            vmem((spans, landing, LANES), BF16),
            vmem((spans, total, LANES), BF16),
            vmem((spans, 8, LANES), F32),
            vmem((spans, ways, 8, LANES), F32),
            vmem((spans, WINDOW, dh), BF16),
            vmem((spans, WINDOW, dh), BF16),
            vmem((out_cols, features), BF16),
            vmem((out_cols, features), BF16),
            vmem((n_head, spans, rows, dh), BF16),
            vmem((spans, rows, dh), F32),
            vmem((spans, rows, dh), F32),
            dma((6 + 2 * spans,)),
            dma((spans, 2, ways)),
            dma((spans, 2, ways)),
            dma((spans, ways)),
            dma((spans, ways)),
            dma((spans, ways)),
            dma((spans, ways)),
            dma((spans, parts, slots)),
            dma((spans, parts, slots)),
            dma((spans, parts, slots)),
            dma((spans, parts, slots)),
            dma((2, spans)),
            dma((2, spans)),
            dma((slots,)),
            dma((slots,)),
            dma((spans, tiles, n_head)),
            dma((spans, tiles, n_head)),
        ],
        compiler_params=pltpu.CompilerParams(
            collective_id=0, has_side_effects=True, vmem_limit_bytes=60 * 1024 * 1024
        ),
    )(
        queries[:, :, 0, :], key_rows[:, :, 0, :], values[:, :, 0, :], learn_rates[0],
        fast_gate[0], fast_down[0], fast_up[0], weight,
    )


def solution(mesh):
    placed = (
        P(None, "seq", "head", None),
        P(None, "seq", "head", None),
        P(None, "seq", "head", None),
        P("head", None, "seq"),
        P("head", None, None),
        P("head", None, None),
        P("head", None, None),
        P(None, ("head", "seq")),
    )
    return jax.shard_map(
        functools.partial(body, mesh.shape["seq"], mesh.shape["head"]),
        mesh=mesh, in_specs=placed, out_specs=P(None, "seq", "head"), check_vma=False,
    )
```
